32 devices in a mesh: cross: 4 (over x, core), along: 8 (over z, y).
Axes of the slice: x: 2, y: 2, z: 4, core: 2. Of those that a mesh axis runs over, the one named last changes fastest.
Arguments:
- surface: float32 [1024, 2048], P('cross', 'along'), may hold values from -6 to 6
- flux_cross: float32 [1024, 2048], P('cross', 'along'), may hold values from -6 to 6
- flux_along: float32 [1024, 2048], P('cross', 'along'), may hold values from -6 to 6
- celerity_sq: float32 [1024, 2048], P('cross', 'along'), may hold values from 0.05 to 1
- wet_mask: int32 [1024, 2048], P('cross', 'along'), may hold values from 0 to 1, as said below
- range_test: float32 [2048, 128], P('along'), may hold values from -0.125 to 0.125
- corange_test: float32 [128, 1024], P(None, 'cross'), may hold values from -0.1875 to 0.1875
- core_left: float32 [256, 1024], P(None, 'cross'), may hold values from -0.1875 to 0.1875
- core_right: float32 [2048, 256], P('along'), may hold values from -0.125 to 0.125
Outputs:
- surface_next: float32 [1024, 2048], P('cross', 'along')
- flux_cross_next: float32 [1024, 2048], P('cross', 'along')
- flux_along_next: float32 [1024, 2048], P('cross', 'along')
- range_sketch: float32 [1024, 128], P('cross')
- corange_sketch: float32 [128, 2048], P(None, 'along')
- core_sketch: float32 [256, 256], replicated
The draws below stay inside these ranges and needn't reach their ends.
Inputs may be any that keep to these rules, and one draw needn't show every extreme that they name: `wet_mask`: 1 marks a wet cell, 0 a dry one.
All inputs are finite; a program needn't handle non-finite values.
Results may differ from the reference program's by a relative error of at most 0.000073.
Values sent between devices are 32-bit elements; how exact they have to be, the bound alone decides.
No kernel may reach another device: no remote copies, remote signals or barrier semaphores. Data moves between devices by JAX's collectives and lax.ppermute only.
A program may use at most 64 MiB of HBM per device.

```python
import math
import jax
import jax.numpy as jnp
from jax import lax

K = 128
S = 256
NX = 1024
NY = 2048


def draw_wet_mask(key, part):
    rows = lax.broadcasted_iota(jnp.int32, (NX, NY), 0)
    limit = 250 + 500 * rows // NX
    picks = jax.random.randint(key, (NX, NY), 0, 1000, dtype=jnp.int32)
    return jnp.where(picks < limit, 1, 0).astype(jnp.int32)


def steps_of(rng, dims, shards, smallest, largest):
    gain = 1.0
    for dim, parts in shards:
        steps = jax.random.uniform(jax.random.fold_in(jax.random.fold_in(rng, 6), dim), (parts,), jnp.float32, smallest / len(shards), largest / len(shards))
        gain = gain * jnp.repeat(jnp.exp(steps), dims[dim] // parts).reshape((-1,) + (1,) * (len(dims) - 1 - dim))
    return gain


def scatter_about(rng, extent, scale, most, cuts=(), kind=jnp.bfloat16):
    values = scale * jax.random.normal(rng, extent, jnp.float32)
    if cuts:
        values = values * steps_of(rng, extent, cuts, -0.22, 0.18)
    return jnp.clip(values, -most, most).astype(kind)


def setup_inputs(seed: int = 0) -> dict:
    key_of = jax.random.split(jax.random.key(seed), 10)
    surface = scatter_about(key_of[0], (NX, NY), 1.0, 6.0, ((0, 4), (1, 8)), jnp.float32)
    flux_cross = scatter_about(key_of[1], (NX, NY), 1.0, 6.0, ((0, 4), (1, 8)), jnp.float32)
    flux_along = scatter_about(key_of[2], (NX, NY), 1.0, 6.0, ((0, 4), (1, 8)), jnp.float32)
    celerity_sq = jnp.clip(jnp.exp(math.log(1.0) - 2.9957323 * jax.random.uniform(key_of[3], (NX, NY), jnp.float32) ** steps_of(key_of[3], (NX, NY), ((0, 4), (1, 8)), -0.2, 0.2)), 0.05, 1.0)
    wet_mask = draw_wet_mask(jax.random.fold_in(key_of[9], 71), 0)
    range_test = scatter_about(key_of[5], (NY, K), NY ** -0.5, 0.125, ((0, 8),), jnp.float32)
    corange_test = scatter_about(key_of[6], (K, NX), NX ** -0.5, 0.1875, ((1, 4),), jnp.float32)
    core_left = scatter_about(key_of[7], (S, NX), NX ** -0.5, 0.1875, ((1, 4),), jnp.float32)
    core_right = scatter_about(key_of[8], (NY, S), NY ** -0.5, 0.125, ((0, 8),), jnp.float32)
    return dict(surface=surface, flux_cross=flux_cross, flux_along=flux_along, celerity_sq=celerity_sq, wet_mask=wet_mask, range_test=range_test, corange_test=corange_test, core_left=core_left, core_right=core_right)


def centred(field, axis):
    widths = [(0, 0), (0, 0)]
    widths[axis] = (2, 2)
    padded = jnp.pad(field, widths)
    count = field.shape[axis]

    def part(start):
        return lax.slice_in_dim(padded, start, start + count, axis=axis)

    return (8.0 * (part(3) - part(1)) - (part(4) - part(0))) / 12.0


def tendency(elev, flux_x, flux_y, wet, celerity_sq):
    masked_x = wet * flux_x
    masked_y = wet * flux_y
    d_elev = -0.25 * wet * (centred(masked_x, 0) + centred(masked_y, 1))
    friction = 0.02 / celerity_sq
    d_flux_x = -wet * (0.25 * celerity_sq * centred(elev, 0) + friction * flux_x)
    d_flux_y = -wet * (0.25 * celerity_sq * centred(elev, 1) + friction * flux_y)
    return d_elev, d_flux_x, d_flux_y


def reference(surface, flux_cross, flux_along, celerity_sq, wet_mask, range_test, corange_test, core_left, core_right):
    wet = wet_mask.astype(jnp.float32)
    k1e, k1p, k1q = tendency(surface, flux_cross, flux_along, wet, celerity_sq)
    k2e, k2p, k2q = tendency(surface + k1e, flux_cross + k1p, flux_along + k1q, wet, celerity_sq)
    surface_next = surface + 0.5 * (k1e + k2e)
    flux_cross_next = flux_cross + 0.5 * (k1p + k2p)
    flux_along_next = flux_along + 0.5 * (k1q + k2q)
    high = lax.Precision.HIGHEST
    range_sketch = jnp.dot(surface_next, range_test, precision=high, preferred_element_type=jnp.float32)
    corange_sketch = jnp.dot(corange_test, surface_next, precision=high, preferred_element_type=jnp.float32)
    right_rows = jnp.dot(surface_next, core_right, precision=high, preferred_element_type=jnp.float32)
    core_sketch = jnp.dot(core_left, right_rows, precision=high, preferred_element_type=jnp.float32)
    return surface_next, flux_cross_next, flux_along_next, range_sketch, corange_sketch, core_sketch
```

```python
import jax
import jax.numpy as jnp
from jax import lax
from jax.sharding import PartitionSpec as P


def with_halo(block, sides, width):
    for axis, dim in sides:
        count = lax.axis_size(axis)
        forward = [(i, i + 1) for i in range(count - 1)]
        backward = [(target, source) for source, target in forward]
        low = lax.ppermute(
            lax.slice_in_dim(block, block.shape[dim] - width, None, axis=dim), axis, forward
        )
        high = lax.ppermute(lax.slice_in_dim(block, 0, width, axis=dim), axis, backward)
        block = jnp.concatenate([low, block, high], axis=dim)
    return block


def derive(padded, axis):
    count = padded.shape[axis] - 4

    def part(start):
        return lax.slice_in_dim(padded, start, start + count, axis=axis)

    return (8.0 * (part(3) - part(1)) - (part(4) - part(0))) / 12.0


def rims(elev, masked_x, masked_y):
    padded_x = with_halo(jnp.stack([elev, masked_x]), (("cross", 1),), 2)
    padded_y = with_halo(jnp.stack([elev, masked_y]), (("along", 2),), 2)
    elev_x = padded_x[0]
    mass_x = padded_x[1]
    elev_y = padded_y[0]
    mass_y = padded_y[1]
    return (elev_x, mass_x, elev_y, mass_y)


def tendency(elev, flux_x, flux_y, wet, celerity_sq):
    masked_x = wet * flux_x
    masked_y = wet * flux_y
    elev_x, mass_x, elev_y, mass_y = rims(elev, masked_x, masked_y)
    d_elev = -0.25 * wet * (derive(mass_x, 0) + derive(mass_y, 1))
    friction = 0.02 / celerity_sq
    d_flux_x = -wet * (0.25 * celerity_sq * derive(elev_x, 0) + friction * flux_x)
    d_flux_y = -wet * (0.25 * celerity_sq * derive(elev_y, 1) + friction * flux_y)
    return (d_elev, d_flux_x, d_flux_y)


AXES = ("cross", "along")
ROWS = 8
LANES = 128


def tiles_of(block):
    down, wide = block.shape[0] // ROWS, block.shape[1] // LANES
    return block.reshape(down, ROWS, wide, LANES).transpose(0, 2, 1, 3)


def block_of(tiles, shape):
    down, wide = shape[0] // ROWS, shape[1] // LANES
    return tiles.reshape(down, wide, ROWS, LANES).transpose(0, 2, 1, 3).reshape(shape)


def sum_sketches(range_part, corange_part, right_part, core_left):
    high = lax.Precision.HIGHEST
    core_part = jnp.dot(core_left, right_part, precision=high, preferred_element_type=jnp.float32)
    crosses, alongs = lax.axis_size("cross"), lax.axis_size("along")
    count = crosses * alongs
    parts = (core_part, range_part, corange_part)
    if any(part.size % (count * ROWS * LANES) for part in parts):
        return (
            lax.psum(range_part, "along"),
            lax.psum(corange_part, "cross"),
            lax.psum(core_part, AXES),
        )
    shares = [tiles_of(part).reshape(count, -1, ROWS, LANES) for part in parts]
    sizes = [share.shape[1] for share in shares]
    cuts = (sizes[0], sizes[0] + sizes[1])
    sent = jnp.concatenate(shares, axis=1)
    got = lax.all_to_all(sent, AXES, 0, 0, tiled=True)
    got = got.reshape((crosses, alongs) + got.shape[1:])
    core, ranged, coranged = jnp.split(got, cuts, axis=2)
    core = jnp.broadcast_to(core.sum((0, 1), keepdims=True), core.shape)
    ranged = jnp.broadcast_to(ranged.sum(1, keepdims=True), ranged.shape)
    coranged = jnp.broadcast_to(coranged.sum(0, keepdims=True), coranged.shape)
    totals = jnp.concatenate([core, ranged, coranged], axis=2).reshape(sent.shape)
    out = lax.all_to_all(totals, AXES, 0, 0, tiled=True)
    core, ranged, coranged = jnp.split(out, cuts, axis=1)
    return (
        block_of(ranged, range_part.shape),
        block_of(coranged, corange_part.shape),
        block_of(core, core_part.shape),
    )


def body(
    surface,
    flux_cross,
    flux_along,
    celerity_sq,
    wet_mask,
    range_test,
    corange_test,
    core_left,
    core_right,
):
    wet = wet_mask.astype(jnp.float32)
    k1e, k1p, k1q = tendency(surface, flux_cross, flux_along, wet, celerity_sq)
    k2e, k2p, k2q = tendency(surface + k1e, flux_cross + k1p, flux_along + k1q, wet, celerity_sq)
    surface_next = surface + 0.5 * (k1e + k2e)
    flux_cross_next = flux_cross + 0.5 * (k1p + k2p)
    flux_along_next = flux_along + 0.5 * (k1q + k2q)
    high = lax.Precision.HIGHEST
    range_part = jnp.dot(
        surface_next, range_test, precision=high, preferred_element_type=jnp.float32
    )
    corange_part = jnp.dot(
        corange_test, surface_next, precision=high, preferred_element_type=jnp.float32
    )
    right_part = jnp.dot(
        surface_next, core_right, precision=high, preferred_element_type=jnp.float32
    )
    range_sketch, corange_sketch, core_sketch = sum_sketches(
        range_part, corange_part, right_part, core_left
    )
    return (
        surface_next,
        flux_cross_next,
        flux_along_next,
        range_sketch,
        corange_sketch,
        core_sketch,
    )


def solution(mesh):
    return jax.shard_map(
        body,
        mesh=mesh,
        in_specs=(
            P("cross", "along"),
            P("cross", "along"),
            P("cross", "along"),
            P("cross", "along"),
            P("cross", "along"),
            P("along", None),
            P(None, "cross"),
            P(None, "cross"),
            P("along", None),
        ),
        out_specs=(
            P("cross", "along"),
            P("cross", "along"),
            P("cross", "along"),
            P("cross", None),
            P(None, "along"),
            P(),
        ),
        check_vma=False,
    )
```

```python
import functools

import jax
import jax.numpy as jnp
from jax import lax
from jax.experimental import pallas as pl
from jax.experimental.pallas import tpu as pltpu
from jax.sharding import PartitionSpec as P

AXES = ("cross", "along")
ROWS = 8
LANES = 128
HIGH = lax.Precision.HIGHEST


def f32(*shape):
    return jax.ShapeDtypeStruct(shape, jnp.float32)


def derive(field, axis):
    size = field.shape[axis]

    def part(shift):
        return pltpu.roll(field, (-shift) % size, axis)

    return (part(1) - part(-1)) * (8.0 / 12.0) - (part(2) - part(-2)) * (1.0 / 12.0)


def coefficients(celerity_sq, wet_mask):
    wet = wet_mask > 0
    return jnp.where(wet, 0.25 * celerity_sq, 0.0), jnp.where(wet, 0.02 / celerity_sq, 0.0)


def friction_of(slope):
    wet = slope > 0.0
    return jnp.where(wet, 0.005 / jnp.where(wet, slope, 1.0), 0.0)


def place(shape, axis, dim):
    return lax.broadcasted_iota(jnp.int32, shape, dim)


def pack_kernel(e_ref, p_ref, q_ref, c_ref, w_ref, even_ref, row0, row1, col0, col1):
    rows, cols = e_ref.shape
    wide = (ROWS, cols)
    at = place(wide, ROWS, 0)
    top = pl.ds(0, ROWS)
    e = e_ref[top, :]
    slope, _ = coefficients(c_ref[top, :], w_ref[top, :])
    mass = jnp.where(w_ref[top, :] > 0, p_ref[top, :], 0.0)
    up = jnp.where(
        at < 4, e, jnp.where(at < 6, pltpu.roll(mass, 4, 0), pltpu.roll(slope, 6, 0))
    )
    end = pl.ds(rows - ROWS, ROWS)
    e = e_ref[end, :]
    slope, _ = coefficients(c_ref[end, :], w_ref[end, :])
    mass = jnp.where(w_ref[end, :] > 0, p_ref[end, :], 0.0)
    down = jnp.where(
        at >= 4, e, jnp.where(at >= 2, pltpu.roll(mass, 4, 0), pltpu.roll(slope, 2, 0))
    )
    even = even_ref[0] == 0
    row0[...] = jnp.where(even, down, up)
    row1[...] = jnp.where(even, up, down)
    first, last = slice(0, LANES), slice(cols - LANES, cols)
    lane = place((rows, LANES), LANES, 1)
    left = lane < LANES // 2

    def edge(ref):
        return jnp.where(left, ref[:, first], ref[:, last])

    e, wet = edge(e_ref), edge(w_ref) > 0
    slope = jnp.where(wet, 0.25 * edge(c_ref), 0.0)
    mass = jnp.where(wet, edge(q_ref), 0.0)
    mass = jnp.where(left, pltpu.roll(mass, 4, 1), pltpu.roll(mass, LANES - 4, 1))
    slope = jnp.where(left, pltpu.roll(slope, 6, 1), pltpu.roll(slope, LANES - 6, 1))
    off = jnp.minimum(lane, LANES - 1 - lane)
    turned = jnp.where(off < 4, e, jnp.where(off < 6, mass, slope)).T
    to_left, to_right = turned[:ROWS], turned[LANES - ROWS :]
    even = even_ref[1] == 0
    col0[...] = jnp.where(even, to_right, to_left)
    col1[...] = jnp.where(even, to_left, to_right)


def row_halo(even, first, second):
    below, above = jnp.where(even, first, second), jnp.where(even, second, first)
    at = place(below.shape, ROWS, 0)

    def pick(count, shift_below, shift_above):
        low = pltpu.roll(below, shift_below, 0) if shift_below else below
        high = pltpu.roll(above, shift_above, 0) if shift_above else above
        return jnp.where(at < count, low, jnp.where(at >= ROWS - count, high, 0.0))

    return pick(4, 0, 0), pick(2, 4, 4), pick(2, 2, 6)


def turn_back(even, first, second):
    right, left = jnp.where(even, first, second), jnp.where(even, second, first)
    gap = jnp.zeros((LANES - 2 * ROWS, right.shape[1]), right.dtype)
    return jnp.concatenate([right, gap, left], axis=0).T


def col_halo(even, first, second):
    both = turn_back(even, first, second)
    lane = place(both.shape, LANES, 1)

    def pick(count, shift):
        low = pltpu.roll(both, LANES - shift, 1) if shift else both
        high = pltpu.roll(both, shift, 1) if shift else both
        return jnp.where(lane < count, low, jnp.where(lane >= LANES - count, high, 0.0))

    return pick(4, 0), pick(2, 4), pick(2, 6)


def dot(a, b):
    return jnp.dot(a, b, precision=HIGH, preferred_element_type=jnp.float32)


def join(tile, halo, axis):
    return jnp.concatenate([tile, halo], axis=axis)


def surface_kernel(
    shared, e_ref, p_ref, q_ref, c_ref, w_ref, even_ref, row0, row1, col0, col1,
    r_ref, cr_ref, left_ref, right_ref, s_ref, fp_ref, fq_ref, *part_refs,
):
    rows, cols = e_ref.shape
    e, p, q = e_ref[...], p_ref[...], q_ref[...]
    wet = w_ref[...] > 0
    slope, friction = coefficients(c_ref[...], w_ref[...])

    def twice(tile_flux, axis, halo):
        halo_e, halo_mass, halo_slope = halo
        grad = derive(join(e, halo_e, axis), axis)
        size = (rows, cols)[axis]
        inner = lax.slice_in_dim(grad, 0, size, axis=axis)
        outer = lax.slice_in_dim(grad, size, grad.shape[axis], axis=axis)
        total = 2.0 * tile_flux - (slope * inner + friction * tile_flux)
        halo_total = (2.0 - friction_of(halo_slope)) * halo_mass - halo_slope * outer
        ring = join(jnp.where(wet, total, 0.0), halo_total, axis)
        next_flux = tile_flux - 0.5 * friction * total
        return lax.slice_in_dim(derive(ring, axis), 0, size, axis=axis), next_flux

    change_x, fp_ref[...] = twice(p, 0, row_halo(even_ref[0] == 0, row0[...], row1[...]))
    change_y, fq_ref[...] = twice(q, 1, col_halo(even_ref[1] == 0, col0[...], col1[...]))
    s = e - jnp.where(wet, 0.125 * (change_x + change_y), 0.0)
    s_ref[...] = s
    ranged = dot(s, r_ref[...])
    coranged = dot(cr_ref[...], s)
    core = dot(left_ref[...], dot(s, right_ref[...]))
    if not shared:
        for ref, value in zip(part_refs, (ranged, coranged, core)):
            ref[...] = value
        return
    (out,) = part_refs
    at = 0
    for part in (core, ranged, coranged):
        for k, tile in enumerate(tiles_of(part)):
            per = tile_count(part) // out.shape[0]
            out[k // per, at + k % per] = tile
        at += per


def tile_count(part):
    return part.shape[0] // ROWS * (part.shape[1] // LANES)


def tile_slices(shape):
    return [
        (slice(i, i + ROWS), slice(j, j + LANES))
        for i in range(0, shape[0], ROWS)
        for j in range(0, shape[1], LANES)
    ]


def tiles_of(part):
    return [part[where] for where in tile_slices(part.shape)]


def sum_kernel(crosses, alongs, cuts, got, out):
    first, second, total = cuts
    count = crosses * alongs

    def add(values):
        values = list(values)
        while len(values) > 1:
            values = [sum(values[i : i + 2][1:], values[i]) for i in range(0, len(values), 2)]
        return values[0]

    for t in range(first):
        value = add(got[k, t] for k in range(count))
        for k in range(count):
            out[k, t] = value
    for t in range(first, second):
        for c in range(crosses):
            value = add(got[c * alongs + a, t] for a in range(alongs))
            for a in range(alongs):
                out[c * alongs + a, t] = value
    for t in range(second, total):
        for a in range(alongs):
            value = add(got[c * alongs + a, t] for c in range(crosses))
            for c in range(crosses):
                out[c * alongs + a, t] = value


def unpack_kernel(got, core, ranged, coranged):
    at = 0
    for ref in (core, ranged, coranged):
        per = tile_count(ref) // got.shape[0]
        for k, where in enumerate(tile_slices(ref.shape)):
            ref[where] = got[k // per, at + k % per]
        at += per


def strip_kernel(e_ref, p_ref, q_ref, w_ref, even_ref, row0, row1, col0, col1,
                 s_ref, both_ref, out_row0, out_row1, out_col0, out_col1):
    del s_ref
    rows, cols = e_ref.shape
    wet = w_ref[...] > 0
    _, mass_rows, _ = row_halo(even_ref[0] == 0, row0[...], row1[...])
    _, mass_cols, _ = col_halo(even_ref[1] == 0, col0[...], col1[...])
    mass_x = jnp.where(wet, p_ref[...], 0.0)
    mass_y = jnp.where(wet, q_ref[...], 0.0)
    spread = derive(join(mass_x, mass_rows, 0), 0)[:rows]
    spread += derive(join(mass_y, mass_cols, 1), 1)[:, :cols]
    both = 2.0 * e_ref[...] - jnp.where(wet, 0.25 * spread, 0.0)
    both_ref[...] = both
    up, down = both[:ROWS], both[rows - ROWS :]
    even = even_ref[0] == 0
    out_row0[...] = jnp.where(even, down, up)
    out_row1[...] = jnp.where(even, up, down)
    lane = place((rows, LANES), LANES, 1)
    turned = jnp.where(lane < LANES // 2, both[:, :LANES], both[:, cols - LANES :]).T
    to_left, to_right = turned[:ROWS], turned[LANES - ROWS :]
    even = even_ref[1] == 0
    out_col0[...] = jnp.where(even, to_right, to_left)
    out_col1[...] = jnp.where(even, to_left, to_right)


def flux_kernel(both_ref, fp_ref, fq_ref, c_ref, w_ref, even_ref, row0, row1, col0, col1,
                p_ref, q_ref):
    rows, cols = both_ref.shape
    both = both_ref[...]
    slope, _ = coefficients(c_ref[...], w_ref[...])
    halo_rows, _, _ = row_halo(even_ref[0] == 0, row0[...], row1[...])
    halo_cols, _, _ = col_halo(even_ref[1] == 0, col0[...], col1[...])
    p_ref[...] = fp_ref[...] - 0.5 * slope * derive(join(both, halo_rows, 0), 0)[:rows]
    q_ref[...] = fq_ref[...] - 0.5 * slope * derive(join(both, halo_cols, 1), 1)[:, :cols]


def exchange(messages):
    moved = []
    for axis, (first, second) in zip(AXES, (messages[:2], messages[2:])):
        count = lax.axis_size(axis)
        for start, message in ((0, first), (1, second)):
            pairs = [(i, i + 1) for i in range(start, count - 1, 2)]
            pairs += [(j, i) for i, j in pairs]
            moved.append(lax.ppermute(message, axis, pairs) if pairs else jnp.zeros_like(message))
    return moved


def body(e, p, q, c, w, range_test, corange_test, core_left, core_right):
    crosses, alongs = lax.axis_size("cross"), lax.axis_size("along")
    count = crosses * alongs
    rows, cols = e.shape
    even = jnp.stack([lax.rem(lax.axis_index(a), 2) for a in AXES])
    strip = [f32(ROWS, cols)] * 2 + [f32(ROWS, rows)] * 2

    def run(kernel, outs, flops, *args):
        kinds = [
            pl.BlockSpec(memory_space=pltpu.SMEM if a is even else pltpu.VMEM) for a in args
        ]
        moved = sum(a.size * a.dtype.itemsize for a in args) + sum(o.size * 4 for o in outs)
        return pl.pallas_call(
            kernel,
            out_shape=outs,
            in_specs=kinds,
            out_specs=[pl.BlockSpec(memory_space=pltpu.VMEM)] * len(outs),
            cost_estimate=pl.CostEstimate(flops=flops, bytes_accessed=moved, transcendentals=0),
            compiler_params=pltpu.CompilerParams(vmem_limit_bytes=32 * 1024 * 1024),
        )(*args)

    cells = rows * cols
    halo = exchange(run(pack_kernel, strip, cells, e, p, q, c, w, even))
    range_shape = f32(rows, range_test.shape[1])
    corange_shape = f32(corange_test.shape[0], cols)
    core_shape = f32(core_left.shape[0], core_right.shape[1])
    shapes = (core_shape, range_shape, corange_shape)
    shared = not any(s.size % (count * ROWS * LANES) for s in shapes)
    tile = f32(rows, cols)
    if shared:
        per = [tile_count(s) // count for s in shapes]
        cuts = (per[0], per[0] + per[1], sum(per))
        sheet = f32(count, cuts[2], ROWS, LANES)
        parts = [sheet]
    else:
        parts = [range_shape, corange_shape, core_shape]
    s_next, half_p, half_q, *parts = run(
        functools.partial(surface_kernel, shared), [tile] * 3 + parts, 800 * cells,
        e, p, q, c, w, even, *halo, range_test, corange_test, core_left, core_right,
    )
    if shared:
        got = lax.all_to_all(parts[0], AXES, 0, 0, tiled=True)
        (totals,) = run(
            functools.partial(sum_kernel, crosses, alongs, cuts), [sheet], sheet.size, got
        )
        handed = lax.all_to_all(totals, AXES, 0, 0, tiled=True)
        core, ranged, coranged = run(unpack_kernel, list(shapes), sheet.size, handed)
    else:
        ranged = lax.psum(parts[0], "along")
        coranged = lax.psum(parts[1], "cross")
        core = lax.psum(parts[2], AXES)
    both, *strips = run(
        strip_kernel, [tile] + strip, 20 * cells, e, p, q, w, even, *halo, s_next
    )
    strips = exchange(strips)
    p_next, q_next = run(
        flux_kernel, [tile] * 2, 20 * cells, both, half_p, half_q, c, w, even, *strips
    )
    return s_next, p_next, q_next, ranged, coranged, core


def solution(mesh):
    tile = P("cross", "along")
    return jax.shard_map(
        body,
        mesh=mesh,
        in_specs=(tile,) * 5
        + (P("along", None), P(None, "cross"), P(None, "cross"), P("along", None)),
        out_specs=(tile,) * 3 + (P("cross", None), P(None, "along"), P()),
        check_vma=False,
    )
```

```python
import functools

import jax
import jax.numpy as jnp
from jax import lax
from jax.experimental import pallas as pl
from jax.experimental.pallas import tpu as pltpu
from jax.sharding import PartitionSpec as P

AXES = ("cross", "along")
ROWS = 8
LANES = 128
HIGH = lax.Precision.HIGHEST


def f32(*shape):
    return jax.ShapeDtypeStruct(shape, jnp.float32)


def derive(field, axis):
    size = field.shape[axis]

    def part(shift):
        return pltpu.roll(field, (-shift) % size, axis)

    return (part(1) - part(-1)) * (8.0 / 12.0) - (part(2) - part(-2)) * (1.0 / 12.0)


def friction_of(slope):
    wet = slope > 0.0
    return jnp.where(wet, 0.005 / jnp.where(wet, slope, 1.0), 0.0)


def place(shape, axis, dim):
    return lax.broadcasted_iota(jnp.int32, shape, dim)


def pack_kernel(e_ref, p_ref, q_ref, a_ref, even_ref, row0, row1, col0, col1):
    rows, cols = e_ref.shape
    at = place((ROWS, cols), ROWS, 0)
    messages = []
    for i, (far, near, turn) in enumerate(((at < 4, at < 6, 6), (at >= 4, at >= 2, 2))):
        here = pl.ds(i * (rows - ROWS), ROWS)
        slope, mass, side = a_ref[here, :], p_ref[here, :], q_ref[here, :]
        first = jnp.where(near, pltpu.roll(mass, 4, 0), pltpu.roll(slope, turn, 0))
        first = jnp.where(far, e_ref[here, :], first)
        messages.append(join(first, jnp.where(far, mass, pltpu.roll(side, 4, 0)), 0))
    up, down = messages
    even = even_ref[0] == 0
    row0[...] = jnp.where(even, down, up)
    row1[...] = jnp.where(even, up, down)
    lane = place((rows, LANES), LANES, 1)
    left = lane < LANES // 2
    off = jnp.minimum(lane, LANES - 1 - lane)

    def edge(ref):
        return jnp.where(left, ref[:, :LANES], ref[:, cols - LANES :])

    def shift(block, count):
        return jnp.where(left, pltpu.roll(block, count, 1), pltpu.roll(block, LANES - count, 1))

    slope, mass, side = edge(a_ref), edge(q_ref), edge(p_ref)
    first = jnp.where(off < 4, edge(e_ref), jnp.where(off < 6, shift(mass, 4), shift(slope, 6))).T
    second = jnp.where(off < 4, mass, shift(side, 4)).T
    to_left = join(first[:ROWS], second[:ROWS], 0)
    to_right = join(first[LANES - ROWS :], second[LANES - ROWS :], 0)
    even = even_ref[1] == 0
    col0[...] = jnp.where(even, to_right, to_left)
    col1[...] = jnp.where(even, to_left, to_right)


def row_pick(even, first, second):
    below, above = jnp.where(even, first, second), jnp.where(even, second, first)
    at = place(below.shape, ROWS, 0)

    def pick(count, shift):
        low = pltpu.roll(below, ROWS - shift, 0) if shift else below
        high = pltpu.roll(above, shift, 0) if shift else above
        return jnp.where(at < count, low, jnp.where(at >= ROWS - count, high, 0.0))

    return pick


def col_pick(even, first, second):
    right, left = jnp.where(even, first, second), jnp.where(even, second, first)
    gap = jnp.zeros((LANES - 2 * ROWS, right.shape[1]), right.dtype)
    both = jnp.concatenate([right, gap, left], axis=0).T
    lane = place(both.shape, LANES, 1)

    def pick(count, shift):
        low = pltpu.roll(both, LANES - shift, 1) if shift else both
        high = pltpu.roll(both, shift, 1) if shift else both
        return jnp.where(lane < count, low, jnp.where(lane >= LANES - count, high, 0.0))

    return pick


def dot(a, b):
    return jnp.dot(a, b, precision=HIGH, preferred_element_type=jnp.float32)


def join(tile, halo, axis):
    return jnp.concatenate([tile, halo], axis=axis)


def surface_kernel(
    e_ref, p_ref, q_ref, a_ref, f_ref, even_ref, row0, row1, col0, col1,
    cr_ref, left_ref, right_ref, s_hbm, s_ref, product_ref, give_ref, corner_ref, sems,
):
    rows, cols = e_ref.shape
    twice_e, slope, friction = e_ref[...], a_ref[...], f_ref[...]

    def change(mass, axis, halo):
        halo_e, halo_mass, halo_slope = halo
        grad = 0.5 * derive(join(twice_e, halo_e, axis), axis)
        size = (rows, cols)[axis]
        inner = lax.slice_in_dim(grad, 0, size, axis=axis)
        outer = lax.slice_in_dim(grad, size, grad.shape[axis], axis=axis)
        total = (2.0 - friction) * mass - slope * inner
        halo_total = (2.0 - friction_of(halo_slope)) * halo_mass - halo_slope * outer
        ring = join(total, halo_total, axis)
        return lax.slice_in_dim(derive(ring, axis), 0, size, axis=axis)

    def halo(pick):
        return pick(4, 0), pick(2, 4), pick(2, 6)

    even_row, even_col = even_ref[0] == 0, even_ref[1] == 0
    pick = row_pick(even_row, row0[:ROWS], row1[:ROWS])
    change_x = change(p_ref[...], 0, halo(pick))
    pick = col_pick(even_col, col0[:ROWS], col1[:ROWS])
    change_y = change(q_ref[...], 1, halo(pick))
    spread = jnp.where(slope > 0.0, 0.125 * (change_x + change_y), 0.0)
    s_ref[...] = 0.5 * twice_e - spread
    part = rows // 4
    copies = [
        pltpu.make_async_copy(s_ref.at[pl.ds(i * part, part), :], s_hbm.at[pl.ds(i * part, part), :], sems.at[i])
        for i in range(4)
    ]
    for copy in copies:
        copy.start()
    s = s_ref[...]
    pick = col_pick(even_col, col0[ROWS:], col1[ROWS:])
    around = join(pick(4, 0), pick(2, 4), 1)
    up, down = around[:ROWS], around[rows - ROWS :]
    give_ref[give_ref.shape[0] - ROWS :, :] = jnp.where(even_row, down, up)
    corner_ref[...] = jnp.where(even_row, up, down)
    product = dot(s, right_ref[...])
    product_ref[...] = product
    give_ref[: give_ref.shape[0] - ROWS, :] = halves(1 - even_ref[0], left_ref, product, cr_ref, s)
    for copy in copies:
        copy.wait()


def halves(side, left_ref, product, cr_ref, s):
    half, thin = left_ref.shape[0] // 2, cr_ref.shape[0] // 2
    core = dot(left_ref[pl.ds(pl.multiple_of(side * half, half), half), :], product)
    coranged = dot(cr_ref[pl.ds(pl.multiple_of(side * thin, thin), thin), :], s)
    return join(core, coranged, 0)


def product_kernel(s_ref, product_ref, even_ref, r_ref, cr_ref, left_ref, keep_ref, range_ref):
    keep_ref[...] = halves(even_ref[0], left_ref, product_ref[...], cr_ref, s_ref[...])
    range_ref[...] = dot(s_ref[...], r_ref[...])


def merge_kernel(half, keep_ref, got_ref, range_ref, out):
    both = keep_ref[...] + got_ref[: keep_ref.shape[0]]
    at = 0
    for part in (both[:half], range_ref[...], both[half:]):
        per = tile_count(part) // out.shape[0]
        for k, tile in enumerate(tiles_of(part)):
            out[k // per, at + k % per] = tile
        at += per


def tile_count(part):
    return part.shape[0] // ROWS * (part.shape[1] // LANES)


def tile_slices(shape):
    return [
        (slice(i, i + ROWS), slice(j, j + LANES))
        for i in range(0, shape[0], ROWS)
        for j in range(0, shape[1], LANES)
    ]


def tiles_of(part):
    return [part[where] for where in tile_slices(part.shape)]


def sum_kernel(crosses, alongs, cuts, got, *rest):
    out = rest[-1]
    first, second, total = cuts
    count = crosses * alongs

    def add(values):
        values = list(values)
        while len(values) > 1:
            values = [sum(values[i : i + 2][1:], values[i]) for i in range(0, len(values), 2)]
        return values[0]

    for t in range(first):
        value = add(got[k, t] for k in range(count))
        for k in range(count):
            out[k, t] = value
    for t in range(first, second):
        for c in range(crosses):
            value = add(got[c * alongs + a, t] for a in range(alongs))
            for a in range(alongs):
                out[c * alongs + a, t] = value
    for t in range(second, total):
        for a in range(alongs):
            value = add(got[c * alongs + a, t] for c in range(crosses))
            for c in range(crosses):
                out[c * alongs + a, t] = value


def unpack_kernel(even_ref, mine, theirs, *refs):
    outs, held, sems = refs[:3], refs[3:6], refs[6]
    count = mine.shape[0]
    even = even_ref[0] == 0
    at = 0
    copies = []
    for out, ref, halved in zip(outs, held, (True, False, True)):
        places = tile_slices(ref.shape)
        keep = len(places) // 2 if halved else len(places)
        per = keep // count
        for k in range(keep):
            tile = mine[k // per, at + k % per]
            if halved:
                other = theirs[k // per, at + k % per]
                ref[places[k]] = jnp.where(even, tile, other)
                ref[places[keep + k]] = jnp.where(even, other, tile)
            else:
                ref[places[k]] = tile
        at += per
        part = ref.shape[0] // 4
        for i in range(0, ref.shape[0], part):
            block = pl.ds(i, part)
            copy = pltpu.make_async_copy(
                ref.at[block, :], out.at[block, :], sems.at[len(copies)]
            )
            copy.start()
            copies.append(copy)
    for copy in copies:
        copy.wait()


def flux_kernel(
    e_ref, mp_ref, mq_ref, a_ref, f_ref, even_ref, row0, row1, col0, col1, got_ref, corner_ref,
    p_ref, q_ref, next_p, next_q, token,
):
    rows, cols = e_ref.shape
    token[...] = jnp.zeros(token.shape, token.dtype)
    twice_e, slope, friction = e_ref[...], a_ref[...], f_ref[...]
    wet = slope > 0.0
    even_row, even_col = even_ref[0] == 0, even_ref[1] == 0
    pick = row_pick(even_row, row0[:ROWS], row1[:ROWS])
    e_rows, wet_rows = pick(4, 0), pick(2, 6) > 0.0
    pick = row_pick(even_row, row0[ROWS:], row1[ROWS:])
    p_rows, q_rows = pick(4, 0), pick(2, 4)
    pick = col_pick(even_col, col0[:ROWS], col1[:ROWS])
    e_cols, wet_cols = pick(4, 0), pick(2, 6) > 0.0
    pick = col_pick(even_col, col0[ROWS:], col1[ROWS:])
    q_cols, p_cols = pick(4, 0), pick(2, 4)
    pick = row_pick(even_row, got_ref[got_ref.shape[0] - ROWS :], corner_ref[...])
    corners = pick(2, 0)
    q_corner, p_corner = corners[:, :LANES], corners[:, LANES:]
    mass_x, mass_y = mp_ref[...], mq_ref[...]
    spread_x = derive(join(mass_x, p_rows, 0), 0)
    spread_y = derive(join(mass_y, q_cols, 1), 1)
    both = twice_e - jnp.where(wet, 0.25 * (spread_x[:rows] + spread_y[:, :cols]), 0.0)
    spread = spread_x[rows:] + derive(join(q_rows, q_corner, 1), 1)[:, :cols]
    both_rows = e_rows - jnp.where(wet_rows, 0.25 * spread, 0.0)
    spread = spread_y[:, cols:] + derive(join(p_cols, p_corner, 0), 0)[:rows]
    both_cols = e_cols - jnp.where(wet_cols, 0.25 * spread, 0.0)

    def step(flux, axis, mass, halo_e, halo_both):
        size = (rows, cols)[axis]
        grad = 0.5 * derive(join(twice_e, halo_e, axis), axis)
        grad = lax.slice_in_dim(grad, 0, size, axis=axis)
        grad_both = derive(join(both, halo_both, axis), axis)
        grad_both = lax.slice_in_dim(grad_both, 0, size, axis=axis)
        total = (2.0 - friction) * mass - slope * grad
        return flux - 0.5 * (slope * grad_both + friction * total)

    next_p[...] = step(p_ref[...], 0, mass_x, e_rows, both_rows)
    next_q[...] = step(q_ref[...], 1, mass_y, e_cols, both_cols)


def pairs_from(start, count):
    pairs = [(i, i + 1) for i in range(start, count - 1, 2)]
    return pairs + [(j, i) for i, j in pairs]


def swap(message, axis, start):
    pairs = pairs_from(start, lax.axis_size(axis))
    return lax.ppermute(message, axis, pairs) if pairs else jnp.zeros_like(message)


def body(e, p, q, c, w, range_test, corange_test, core_left, core_right):
    crosses, alongs = lax.axis_size("cross"), lax.axis_size("along")
    rows, cols = e.shape
    cells = rows * cols
    even = jnp.stack([lax.rem(lax.axis_index(a), 2) for a in AXES])

    def run(kernel, outs, flops, *args, idle=(), scratch=(), to=None):
        kinds = [pl.BlockSpec(memory_space=pltpu.SMEM if a is even else pltpu.VMEM) for a in args]
        kinds += [pl.BlockSpec(memory_space=pl.ANY)] * len(idle)
        moved = sum(a.size * 4 for a in args) + sum(o.size * 4 for o in outs)
        to = to or [pltpu.VMEM] * len(outs)
        return pl.pallas_call(
            kernel,
            out_shape=outs,
            in_specs=kinds,
            out_specs=[pl.BlockSpec(memory_space=kind) for kind in to],
            scratch_shapes=list(scratch),
            cost_estimate=pl.CostEstimate(flops=flops, bytes_accessed=moved, transcendentals=0),
            compiler_params=pltpu.CompilerParams(vmem_limit_bytes=32 * 1024 * 1024),
        )(*args, *idle)

    wet = w > 0
    slope = jnp.where(wet, 0.25 * c, 0.0)
    friction = jnp.where(wet, 0.02 / c, 0.0)
    mass_x, mass_y = jnp.where(wet, p, 0.0), jnp.where(wet, q, 0.0)
    twice_e = e + e
    strip = [f32(2 * ROWS, cols)] * 2 + [f32(2 * ROWS, rows)] * 2
    halo = run(pack_kernel, strip, cells, twice_e, mass_x, mass_y, slope, even)
    order = (3, 1, 2, 0)
    moved = {i: swap(halo[i], AXES[i // 2], i % 2) for i in order}
    halo = [moved[i] for i in range(4)]
    fields = (twice_e, mass_x, mass_y, slope, friction)
    range_shape = f32(rows, range_test.shape[1])
    corange_shape = f32(corange_test.shape[0], cols)
    core_shape = f32(core_left.shape[0], core_right.shape[1])
    tile = f32(rows, cols)
    half, thin = core_shape.shape[0] // 2, corange_shape.shape[0] // 2
    outs = [tile] * 2 + [f32(rows, core_shape.shape[1])]
    outs += [f32(half + thin + ROWS, cols), f32(ROWS, 2 * LANES)]
    s_next, s_held, product, give, corner = run(
        surface_kernel, outs, 600 * cells,
        *fields, even, *halo, corange_test, core_left, core_right,
        to=[pltpu.HBM] + [pltpu.VMEM] * 4, scratch=[pltpu.SemaphoreType.DMA((4,))],
    )
    got = swap(give, "cross", 0)
    corner = swap(corner, "cross", 1)
    p_next, q_next, token = run(
        flux_kernel, [tile] * 2 + [f32(ROWS, LANES)], 80 * cells, *fields, even, *halo, got, corner, p, q
    )
    count = crosses // 2 * alongs
    sizes = (half * core_shape.shape[1], range_shape.size, thin * cols)
    if crosses % 2 == 0 and not any(size % (count * ROWS * LANES) for size in sizes):
        per = [size // (count * ROWS * LANES) for size in sizes]
        cuts = (per[0], per[0] + per[1], sum(per))
        sheet = f32(count, cuts[2], ROWS, LANES)
        groups = [
            [i * alongs + a for i in range(side, crosses, 2) for a in range(alongs)]
            for side in range(2)
        ]

        def spread(x):
            return lax.all_to_all(x, AXES, 0, 0, tiled=True, axis_index_groups=groups)

        keep, ranged = run(
            product_kernel, [f32(half + thin, cols), range_shape], 300 * cells,
            s_held, product, even, range_test, corange_test, core_left,
        )
        (shares,) = run(
            functools.partial(merge_kernel, half), [sheet], sheet.size, keep, got, ranged
        )
        (totals,) = run(
            functools.partial(sum_kernel, crosses // 2, alongs, cuts), [sheet], sheet.size,
            spread(shares), idle=[token],
        )
        mine = spread(totals)
        theirs = swap(mine, "cross", 0)
        shapes = [core_shape, range_shape, corange_shape]
        core, ranged, coranged = run(
            unpack_kernel, shapes, sheet.size, even, mine, theirs, to=[pltpu.HBM] * 3,
            scratch=[pltpu.VMEM(x.shape, x.dtype) for x in shapes]
            + [pltpu.SemaphoreType.DMA((12,))],
        )
    else:
        ranged = lax.psum(dot(s_held, range_test), "along")
        coranged = lax.psum(dot(corange_test, s_held), "cross")
        core = lax.psum(dot(core_left, product), AXES)
    return s_next, p_next, q_next, ranged, coranged, core


def solution(mesh):
    tile = P("cross", "along")
    return jax.shard_map(
        body,
        mesh=mesh,
        in_specs=(tile,) * 5
        + (P("along", None), P(None, "cross"), P(None, "cross"), P("along", None)),
        out_specs=(tile,) * 3 + (P("cross", None), P(None, "along"), P()),
        check_vma=False,
    )
```

```python
import functools

import jax
import jax.numpy as jnp
from jax import lax
from jax.experimental import pallas as pl
from jax.experimental.pallas import tpu as pltpu
from jax.sharding import PartitionSpec as P

AXES = ("cross", "along")
ROWS = 8
LANES = 128
WINDOW = 64


def f32(*shape):
    return jax.ShapeDtypeStruct(shape, jnp.float32)


def derive(field, axis):
    size = field.shape[axis]

    def part(shift):
        return pltpu.roll(field, (-shift) % size, axis)

    return (part(1) - part(-1)) * (8.0 / 12.0) - (part(2) - part(-2)) * (1.0 / 12.0)


def friction_of(slope):
    wet = slope > 0.0
    return jnp.where(wet, 0.005 / jnp.where(wet, slope, 1.0), 0.0)


def place(shape, axis, dim):
    return lax.broadcasted_iota(jnp.int32, shape, dim)


def parity(axis):
    return lax.rem(lax.axis_index(axis), 2)


def row_kernel(e_hbm, p_hbm, q_hbm, c_hbm, w_hbm, first_ref, second_ref, eb, pb, qb, cb, wb, sems):
    rows, cols = e_hbm.shape
    copies = [
        pltpu.make_async_copy(source.at[pl.ds(i * (rows - ROWS), ROWS), :], to.at[i], sems.at[k, i])
        for k, (source, to) in enumerate(
            ((e_hbm, eb), (p_hbm, pb), (q_hbm, qb), (c_hbm, cb), (w_hbm, wb))
        )
        for i in range(2)
    ]
    for copy in copies:
        copy.start()
    for copy in copies:
        copy.wait()
    at = place((ROWS, cols), ROWS, 0)
    messages = []
    for i, (far, near, turn) in enumerate(((at < 4, at < 6, 6), (at >= 4, at >= 2, 2))):
        wet = wb[i] > 0
        slope = jnp.where(wet, 0.25 * cb[i], 0.0)
        mass, side = jnp.where(wet, pb[i], 0.0), jnp.where(wet, qb[i], 0.0)
        first = jnp.where(near, pltpu.roll(mass, 4, 0), pltpu.roll(slope, turn, 0))
        first = jnp.where(far, 2.0 * eb[i], first)
        messages.append(join(first, jnp.where(far, mass, pltpu.roll(side, 4, 0)), 0))
    up, down = messages
    even = parity("cross") == 0
    first_ref[...] = jnp.where(even, down, up)
    second_ref[...] = jnp.where(even, up, down)


def col_kernel(
    e_in, p_in, q_in, c_in, w_in, e_ref, p_ref, q_ref, a_ref, f_ref, first_ref, second_ref
):
    rows, cols = e_ref.shape
    for start, step in windows(rows):
        here = slice(start, start + step)
        wet, celerity_sq = w_in[here, :] > 0, c_in[here, :]
        e_ref[here, :] = 2.0 * e_in[here, :]
        p_ref[here, :] = jnp.where(wet, p_in[here, :], 0.0)
        q_ref[here, :] = jnp.where(wet, q_in[here, :], 0.0)
        a_ref[here, :] = jnp.where(wet, 0.25 * celerity_sq, 0.0)
        f_ref[here, :] = jnp.where(wet, 0.02 / celerity_sq, 0.0)
    lane = place((rows, LANES), LANES, 1)
    left = lane < LANES // 2
    off = jnp.minimum(lane, LANES - 1 - lane)

    def edge(ref):
        return jnp.where(left, ref[:, :LANES], ref[:, cols - LANES :])

    def shift(block, count):
        return jnp.where(left, pltpu.roll(block, count, 1), pltpu.roll(block, LANES - count, 1))

    slope, mass, side = edge(a_ref), edge(q_ref), edge(p_ref)
    first = jnp.where(off < 4, edge(e_ref), jnp.where(off < 6, shift(mass, 4), shift(slope, 6))).T
    second = jnp.where(off < 4, mass, shift(side, 4)).T
    to_left = join(first[:ROWS], second[:ROWS], 0)
    to_right = join(first[LANES - ROWS :], second[LANES - ROWS :], 0)
    even = parity("along") == 0
    first_ref[...] = jnp.where(even, to_right, to_left)
    second_ref[...] = jnp.where(even, to_left, to_right)


def row_pick(even, first, second):
    below, above = jnp.where(even, first, second), jnp.where(even, second, first)
    at = place(below.shape, ROWS, 0)

    def pick(count, shift):
        low = pltpu.roll(below, ROWS - shift, 0) if shift else below
        high = pltpu.roll(above, shift, 0) if shift else above
        return jnp.where(at < count, low, jnp.where(at >= ROWS - count, high, 0.0))

    return pick


def col_pick(even, first, second):
    right, left = jnp.where(even, first, second), jnp.where(even, second, first)
    gap = jnp.zeros((LANES - 2 * ROWS, right.shape[1]), right.dtype)
    both = jnp.concatenate([right, gap, left], axis=0).T
    lane = place(both.shape, LANES, 1)

    def pick(count, shift):
        low = pltpu.roll(both, LANES - shift, 1) if shift else both
        high = pltpu.roll(both, shift, 1) if shift else both
        return jnp.where(lane < count, low, jnp.where(lane >= LANES - count, high, 0.0))

    return pick


def split(a):
    high = a.astype(jnp.bfloat16)
    return high, (a - high.astype(jnp.float32)).astype(jnp.bfloat16)


def dot_split(a, b):
    (a_high, a_low), (b_high, b_low) = a, b

    def product(x, y):
        return jnp.dot(x, y, preferred_element_type=jnp.float32)

    return product(a_high, b_high) + (product(a_high, b_low) + product(a_low, b_high))


def dot(a, b):
    return dot_split(split(a), split(b))


def join(tile, halo, axis):
    return jnp.concatenate([tile, halo], axis=axis)


def windows(rows):
    step = WINDOW if rows % WINDOW == 0 else ROWS
    for start in range(0, rows, step):
        yield start, step


def with_ring(part, ring, start, step, rows):
    parts = [part]
    if start == 0:
        parts.insert(0, ring)
    if start + step == rows:
        parts.append(ring)
    return jnp.concatenate(parts, axis=0) if len(parts) > 1 else part


def window(tile, ring, start, step):
    rows = tile.shape[0]
    part = tile[max(start - ROWS, 0) : min(start + step + ROWS, rows)]
    return with_ring(part, ring, start, step, rows)


def surface_kernel(
    e_ref, p_ref, q_ref, a_ref, f_ref, row1, row0, col1, col0,
    cr_ref, left_ref, right_ref, s_ref, sum_p, sum_q, product_ref, give_ref,
):
    rows, cols = e_ref.shape
    even_row, even_col = parity("cross") == 0, parity("along") == 0

    def halo(pick):
        e, mass, slope = pick(4, 0), pick(2, 4), pick(2, 6)
        return e, (2.0 - friction_of(slope)) * mass, slope

    e_row, g_row, a_row = halo(row_pick(even_row, row0[:ROWS], row1[:ROWS]))
    e_col, g_col, a_col = halo(col_pick(even_col, col0[:ROWS], col1[:ROWS]))
    for start, step in windows(rows):
        inner = slice(start, start + step)
        grad = derive(window(e_ref, e_row, start, step), 0)
        slope = window(a_ref, a_row, start, step)
        around = slice(max(start - ROWS, 0), min(start + step + ROWS, rows))
        total = with_ring((2.0 - f_ref[around, :]) * p_ref[around, :], g_row, start, step, rows)
        total -= 0.5 * slope * grad
        sum_p[inner, :] = total[ROWS : ROWS + step]
        change = derive(total, 0)[ROWS : ROWS + step]
        grad = derive(join(e_ref[inner, :], e_col[inner], 1), 1)
        slope = a_ref[inner, :]
        total = (2.0 - f_ref[inner, :]) * q_ref[inner, :]
        total = join(total, g_col[inner], 1) - 0.5 * join(slope, a_col[inner], 1) * grad
        sum_q[inner, :] = total[:, :cols]
        change += derive(total, 1)[:, :cols]
        s_ref[inner, :] = 0.5 * e_ref[inner, :] - jnp.where(slope > 0.0, 0.125 * change, 0.0)
    s = split(s_ref[...])
    pick = col_pick(even_col, col0[ROWS:], col1[ROWS:])
    around = join(pick(4, 0), pick(2, 4), 1)
    up, down = around[:ROWS], around[rows - ROWS :]
    tail = give_ref.shape[0] - 2 * ROWS
    give_ref[tail:, :] = jnp.where(even_row, join(down, up, 0), join(up, down, 0))
    product = dot_split(s, split(right_ref[...]))
    product_ref[...] = product
    give_ref[:tail, :] = halves(
        1 - parity("cross"), left_ref, split(product), cr_ref, s
    )


def halves(side, left_ref, product, cr_ref, s):
    half, thin = left_ref.shape[0] // 2, cr_ref.shape[0] // 2
    left = left_ref[pl.ds(pl.multiple_of(side * half, half), half), :]
    core = dot_split(split(left), product)
    thin_rows = cr_ref[pl.ds(pl.multiple_of(side * thin, thin), thin), :]
    return join(core, dot_split(split(thin_rows), s), 0)


def product_kernel(
    s_ref, product_ref, r_ref, cr_ref, left_ref, s_hbm, keep_ref, range_ref, sems
):
    copies = start(pieces(s_ref, s_hbm, sems))
    s = split(s_ref[...])
    keep_ref[...] = halves(parity("cross"), left_ref, split(product_ref[...]), cr_ref, s)
    range_ref[...] = dot_split(s, split(r_ref[...]))
    for copy in copies:
        copy.wait()


def start(copies):
    for copy in copies:
        copy.start()
    return copies


def pieces(source, to, sems, count=4):
    part = source.shape[0] // count
    blocks = [pl.ds(i * part, part) for i in range(count)]
    return [
        pltpu.make_async_copy(source.at[block, :], to.at[block, :], sems.at[i])
        for i, block in enumerate(blocks)
    ]


def merge_kernel(half, keep_ref, got_ref, range_ref, out, across_ref):
    ends = keep_ref.shape[0]
    both = keep_ref[...] + got_ref[:ends]
    at = 0
    for part in (both[:half], range_ref[...]):
        per = tile_count(part) // out.shape[0]
        for k, tile in enumerate(tiles_of(part)):
            out[k // per, at + k % per] = tile
        at += per
    across_ref[...] = join(both[half:], got_ref[ends + ROWS :], 0)


def tile_count(part):
    return part.shape[0] // ROWS * (part.shape[1] // LANES)


def tile_slices(shape):
    return [
        (slice(i, i + ROWS), slice(j, j + LANES))
        for i in range(0, shape[0], ROWS)
        for j in range(0, shape[1], LANES)
    ]


def tiles_of(part):
    return [part[where] for where in tile_slices(part.shape)]


def sum_kernel(crosses, alongs, cuts, got, *rest):
    out = rest[-1]
    first, second = cuts
    count = crosses * alongs

    def add(values):
        values = list(values)
        while len(values) > 1:
            values = [sum(values[i : i + 2][1:], values[i]) for i in range(0, len(values), 2)]
        return values[0]

    for t in range(first):
        value = add(got[k, t] for k in range(count))
        for k in range(count):
            out[k, t] = value
    for t in range(first, second):
        for c in range(crosses):
            value = add(got[c * alongs + a, t] for a in range(alongs))
            for a in range(alongs):
                out[c * alongs + a, t] = value


def unpack_kernel(mine, theirs, thin_mine, thin_theirs, *refs):
    outs, held, sems = refs[:3], refs[3:6], refs[6]
    core, ranged, coranged = held
    count = mine.shape[0]
    even = parity("cross") == 0
    thin = thin_mine.shape[0]
    coranged[:thin] = jnp.where(even, thin_mine[...], thin_theirs[...])
    coranged[thin:] = jnp.where(even, thin_theirs[...], thin_mine[...])
    copies = start(pieces(coranged, outs[2], sems.at[2]))
    places = tile_slices(ranged.shape)
    wide = len(tile_slices(core.shape)) // 2 // count
    per = len(places) // count
    for k, where in enumerate(places):
        ranged[where] = mine[k // per, wide + k % per]
    copies += start(pieces(ranged, outs[1], sems.at[1]))
    places = tile_slices(core.shape)
    keep = len(places) // 2
    for k in range(keep):
        tile, other = mine[k // wide, k % wide], theirs[k // wide, k % wide]
        core[places[k]] = jnp.where(even, tile, other)
        core[places[keep + k]] = jnp.where(even, other, tile)
    copies += start(pieces(core, outs[0], sems.at[0]))
    for copy in copies:
        copy.wait()


def flux_kernel(
    e_ref, mp_ref, mq_ref, a_ref, f_ref, row1, row0, col1, col0, got_ref, corner_ref,
    p_ref, q_ref, sum_p, sum_q, p_hbm, q_hbm, next_p, next_q, sems,
):
    rows, cols = e_ref.shape
    copies = []
    even_row, even_col = parity("cross") == 0, parity("along") == 0
    pick = row_pick(even_row, row0[:ROWS], row1[:ROWS])
    e_row, a_row = pick(4, 0), pick(2, 6)
    pick = row_pick(even_row, row0[ROWS:], row1[ROWS:])
    p_row, q_row = pick(4, 0), pick(2, 4)
    pick = col_pick(even_col, col0[:ROWS], col1[:ROWS])
    e_col, a_col = pick(4, 0), pick(2, 6)
    pick = col_pick(even_col, col0[ROWS:], col1[ROWS:])
    q_col, p_col = pick(4, 0), pick(2, 4)
    row = lax.axis_index("cross")
    inside = (row > 0) & (row < lax.axis_size("cross") - 1)
    beyond = jnp.where(inside, corner_ref[corner_ref.shape[0] - ROWS :], 0.0)
    near = got_ref.shape[0] - 2 * ROWS
    pick = row_pick(even_row, got_ref[near : near + ROWS], beyond)
    corners = pick(2, 0)
    none = jnp.zeros((ROWS, LANES), e_ref.dtype)
    for i, (start, step) in enumerate(windows(rows)):

        def ring(tile, row, col, corner):
            return join(
                window(tile, row, start, step), window(col, corner, start, step), 1
            )

        spread = derive(ring(mp_ref, p_row, p_col, corners[:, LANES:]), 0)
        spread += derive(ring(mq_ref, q_row, q_col, corners[:, :LANES]), 1)
        wet = ring(a_ref, a_row, a_col, none) > 0.0
        both = ring(e_ref, e_row, e_col, none) - jnp.where(wet, 0.25 * spread, 0.0)
        inner = slice(start, start + step)
        grad_x = derive(both[:, :cols], 0)[ROWS : ROWS + step]
        grad_y = derive(both[ROWS : ROWS + step], 1)[:, :cols]
        slope, friction = 0.5 * a_ref[inner, :], 0.5 * f_ref[inner, :]
        next_p[inner, :] = p_ref[inner, :] - (slope * grad_x + friction * sum_p[inner, :])
        next_q[inner, :] = q_ref[inner, :] - (slope * grad_y + friction * sum_q[inner, :])
        for k, (ref, hbm) in enumerate(((next_p, p_hbm), (next_q, q_hbm))):
            copy = pltpu.make_async_copy(ref.at[inner, :], hbm.at[inner, :], sems.at[k, i])
            copy.start()
            copies.append(copy)
    for copy in copies:
        copy.wait()


def pairs_from(start, count):
    pairs = [(i, i + 1) for i in range(start, count - 1, 2)]
    return pairs + [(j, i) for i, j in pairs]


def swap(message, axis, start):
    pairs = pairs_from(start, lax.axis_size(axis))
    return lax.ppermute(message, axis, pairs) if pairs else jnp.zeros_like(message)


def body(e, p, q, c, w, range_test, corange_test, core_left, core_right):
    crosses, alongs = lax.axis_size("cross"), lax.axis_size("along")
    rows, cols = e.shape
    cells = rows * cols

    def run(kernel, outs, flops, *args, idle=(), scratch=(), to=None, space=pltpu.VMEM, limit=32):
        kinds = [pl.BlockSpec(memory_space=space)] * len(args)
        kinds += [pl.BlockSpec(memory_space=pl.ANY)] * len(idle)
        moved = sum(a.size * 4 for a in args) + sum(o.size * 4 for o in outs)
        to = to or [pltpu.VMEM] * len(outs)
        return pl.pallas_call(
            kernel,
            out_shape=outs,
            in_specs=kinds,
            out_specs=[pl.BlockSpec(memory_space=kind) for kind in to],
            scratch_shapes=list(scratch),
            cost_estimate=pl.CostEstimate(flops=flops, bytes_accessed=moved, transcendentals=0),
            compiler_params=pltpu.CompilerParams(vmem_limit_bytes=limit * 1024 * 1024),
        )(*args, *idle)

    held = [pltpu.VMEM((2, ROWS, cols), a.dtype) for a in (e, p, q, c, w)]
    row0, row1 = run(
        row_kernel, [f32(2 * ROWS, cols)] * 2, cells, e, p, q, c, w, space=pltpu.HBM,
        scratch=held + [pltpu.SemaphoreType.DMA((5, 2))], limit=60,
    )
    row1, row0 = swap(row1, "cross", 1), swap(row0, "cross", 0)
    tile = f32(rows, cols)
    *fields, col0, col1 = run(
        col_kernel, [tile] * 5 + [f32(2 * ROWS, rows)] * 2, 10 * cells, e, p, q, c, w
    )
    col1, col0 = swap(col1, "along", 1), swap(col0, "along", 0)
    halo = (row1, row0, col1, col0)
    range_shape = f32(rows, range_test.shape[1])
    corange_shape = f32(corange_test.shape[0], cols)
    core_shape = f32(core_left.shape[0], core_right.shape[1])
    half, thin = core_shape.shape[0] // 2, corange_shape.shape[0] // 2
    outs = [tile] * 3 + [f32(rows, core_shape.shape[1])]
    outs += [f32(half + thin + 2 * ROWS, cols)]
    s_held, sum_p, sum_q, product, give = run(
        surface_kernel, outs, 600 * cells,
        *fields, *halo, corange_test, core_left, core_right,
    )
    got = swap(give, "cross", 0)
    count = crosses // 2 * alongs
    sizes = (half * core_shape.shape[1], range_shape.size)
    keep_shape = f32(half + thin, cols)
    s_next, keep, ranged = run(
        product_kernel, [tile, keep_shape, range_shape], 300 * cells,
        s_held, product, range_test, corange_test, core_left,
        to=[pltpu.HBM, pltpu.VMEM, pltpu.VMEM], scratch=[pltpu.SemaphoreType.DMA((4,))],
    )
    shared = crosses == 4 and not any(size % (count * ROWS * LANES) for size in sizes)
    if shared:
        per = [size // (count * ROWS * LANES) for size in sizes]
        cuts = (per[0], per[0] + per[1])
        sheet = f32(count, cuts[1], ROWS, LANES)
        groups = [
            [i * alongs + a for i in range(side, crosses, 2) for a in range(alongs)]
            for side in range(2)
        ]

        def spread(x):
            return lax.all_to_all(x, AXES, 0, 0, tiled=True, axis_index_groups=groups)

        shares, across = run(
            functools.partial(merge_kernel, half), [sheet, f32(thin + ROWS, cols)], sheet.size,
            keep, got, ranged,
        )
        corner = lax.ppermute(across, "cross", [(i, i ^ 2) for i in range(crosses)])
        thin_mine = across[:thin] + corner[:thin]
        thin_theirs = swap(thin_mine, "cross", 0)
        (totals,) = run(
            functools.partial(sum_kernel, crosses // 2, alongs, cuts), [sheet], sheet.size,
            spread(shares), idle=[thin_mine],
        )
        mine = spread(totals)
        theirs = swap(mine, "cross", 0)
        shapes = [core_shape, range_shape, corange_shape]
        core, ranged, coranged = run(
            unpack_kernel, shapes, sheet.size, mine, theirs, thin_mine, thin_theirs,
            to=[pltpu.HBM] * 3,
            scratch=[pltpu.VMEM(x.shape, x.dtype) for x in shapes]
            + [pltpu.SemaphoreType.DMA((3, 4))],
        )
    else:
        corner = swap(give[-ROWS:], "cross", 1)
        ranged = lax.psum(ranged, "along")
        coranged = lax.psum(dot(corange_test, s_held), "cross")
        core = lax.psum(dot(core_left, product), AXES)
    p_next, q_next = run(
        flux_kernel, [tile] * 2, 80 * cells, *fields, *halo, got, corner, p, q, sum_p, sum_q,
        to=[pltpu.HBM] * 2,
        scratch=[pltpu.VMEM((rows, cols), jnp.float32)] * 2
        + [pltpu.SemaphoreType.DMA((2, len(list(windows(rows)))))],
    )
    return s_next, p_next, q_next, ranged, coranged, core


def solution(mesh):
    tile = P("cross", "along")
    return jax.shard_map(
        body,
        mesh=mesh,
        in_specs=(tile,) * 5
        + (P("along", None), P(None, "cross"), P(None, "cross"), P("along", None)),
        out_specs=(tile,) * 3 + (P("cross", None), P(None, "along"), P()),
        check_vma=False,
    )
```

```python
import functools

import jax
import jax.numpy as jnp
from jax import lax
from jax.experimental import pallas as pl
from jax.experimental.pallas import tpu as pltpu
from jax.sharding import PartitionSpec as P

AXES = ("cross", "along")
ROWS = 8
LANES = 128
WINDOW = 64
ROOM = 56_450_000


def f32(*shape):
    return jax.ShapeDtypeStruct(shape, jnp.float32)


def derive(field, axis):
    size = field.shape[axis]

    def part(shift):
        return pltpu.roll(field, (-shift) % size, axis)

    return (part(1) - part(-1)) * (8.0 / 12.0) - (part(2) - part(-2)) * (1.0 / 12.0)


def friction_of(slope):
    wet = slope > 0.0
    return jnp.where(wet, 0.005 / jnp.where(wet, slope, 1.0), 0.0)


def place(shape, axis, dim):
    return lax.broadcasted_iota(jnp.int32, shape, dim)


def parity(axis):
    return lax.rem(lax.axis_index(axis), 2)


def row_kernel(e_hbm, p_hbm, q_hbm, c_hbm, w_hbm, first_ref, second_ref, eb, pb, qb, cb, wb, sems):
    rows, cols = e_hbm.shape
    copies = [
        pltpu.make_async_copy(source.at[pl.ds(i * (rows - ROWS), ROWS), :], to.at[i], sems.at[k, i])
        for k, (source, to) in enumerate(
            ((e_hbm, eb), (p_hbm, pb), (q_hbm, qb), (c_hbm, cb), (w_hbm, wb))
        )
        for i in range(2)
    ]
    for copy in copies:
        copy.start()
    for copy in copies:
        copy.wait()
    at = place((ROWS, cols), ROWS, 0)
    messages = []
    for i, (far, near, turn) in enumerate(((at < 4, at < 6, 6), (at >= 4, at >= 2, 2))):
        wet = wb[i] > 0
        slope = jnp.where(wet, 0.25 * cb[i], 0.0)
        mass, side = jnp.where(wet, pb[i], 0.0), jnp.where(wet, qb[i], 0.0)
        first = jnp.where(near, pltpu.roll(mass, 4, 0), pltpu.roll(slope, turn, 0))
        first = jnp.where(far, 2.0 * eb[i], first)
        messages.append(join(first, jnp.where(far, mass, pltpu.roll(side, 4, 0)), 0))
    up, down = messages
    even = parity("cross") == 0
    first_ref[...] = jnp.where(even, down, up)
    second_ref[...] = jnp.where(even, up, down)


def col_kernel(
    e_in, p_in, q_in, c_in, w_in, e_ref, p_ref, q_ref, a_ref, f_ref, first_ref, second_ref
):
    rows, cols = e_ref.shape
    for start, step in windows(rows):
        here = slice(start, start + step)
        wet, celerity_sq = w_in[here, :] > 0, c_in[here, :]
        e_ref[here, :] = 2.0 * e_in[here, :]
        p_ref[here, :] = jnp.where(wet, p_in[here, :], 0.0)
        q_ref[here, :] = jnp.where(wet, q_in[here, :], 0.0)
        a_ref[here, :] = jnp.where(wet, 0.25 * celerity_sq, 0.0)
        f_ref[here, :] = jnp.where(wet, 0.02 / celerity_sq, 0.0)
    lane = place((rows, LANES), LANES, 1)
    left = lane < LANES // 2
    off = jnp.minimum(lane, LANES - 1 - lane)

    def edge(ref):
        return jnp.where(left, ref[:, :LANES], ref[:, cols - LANES :])

    def shift(block, count):
        return jnp.where(left, pltpu.roll(block, count, 1), pltpu.roll(block, LANES - count, 1))

    slope, mass, side = edge(a_ref), edge(q_ref), edge(p_ref)
    first = jnp.where(off < 4, edge(e_ref), jnp.where(off < 6, shift(mass, 4), shift(slope, 6))).T
    second = jnp.where(off < 4, mass, shift(side, 4)).T
    to_left = join(first[:ROWS], second[:ROWS], 0)
    to_right = join(first[LANES - ROWS :], second[LANES - ROWS :], 0)
    even = parity("along") == 0
    first_ref[...] = jnp.where(even, to_right, to_left)
    second_ref[...] = jnp.where(even, to_left, to_right)


def row_pick(even, first, second):
    below, above = jnp.where(even, first, second), jnp.where(even, second, first)
    at = place(below.shape, ROWS, 0)

    def pick(count, shift):
        low = pltpu.roll(below, ROWS - shift, 0) if shift else below
        high = pltpu.roll(above, shift, 0) if shift else above
        return jnp.where(at < count, low, jnp.where(at >= ROWS - count, high, 0.0))

    return pick


def turn_back(even, first, second):
    right, left = jnp.where(even, first, second), jnp.where(even, second, first)
    gap = jnp.zeros((LANES - 2 * ROWS, right.shape[1]), right.dtype)
    return jnp.concatenate([right, gap, left], axis=0).T


def lane_pick(both):
    lane = place(both.shape, LANES, 1)

    def pick(count, shift):
        low = pltpu.roll(both, LANES - shift, 1) if shift else both
        high = pltpu.roll(both, shift, 1) if shift else both
        return jnp.where(lane < count, low, jnp.where(lane >= LANES - count, high, 0.0))

    return pick


def col_pick(even, first, second):
    return lane_pick(turn_back(even, first, second))


def split(a):
    high = a.astype(jnp.bfloat16)
    return high, (a - high.astype(jnp.float32)).astype(jnp.bfloat16)


def dot_split(a, b):
    (a_high, a_low), (b_high, b_low) = a, b

    def product(x, y):
        return jnp.dot(x, y, preferred_element_type=jnp.float32)

    return product(a_high, b_high) + (product(a_high, b_low) + product(a_low, b_high))


def dot(a, b):
    return dot_split(split(a), split(b))


def join(tile, halo, axis):
    return jnp.concatenate([tile, halo], axis=axis)


def windows(rows):
    step = WINDOW if rows % WINDOW == 0 else ROWS
    for start in range(0, rows, step):
        yield start, step


def with_ring(part, ring, start, step, rows):
    parts = [part]
    if start == 0:
        parts.insert(0, ring)
    if start + step == rows:
        parts.append(ring)
    return jnp.concatenate(parts, axis=0) if len(parts) > 1 else part


def window(tile, ring, start, step):
    rows = tile.shape[0]
    part = tile[max(start - ROWS, 0) : min(start + step + ROWS, rows)]
    return with_ring(part, ring, start, step, rows)


def halo_of(pick):
    e, mass, slope = pick(4, 0), pick(2, 4), pick(2, 6)
    return e, (2.0 - friction_of(slope)) * mass, slope


def inner_kernel(
    e_ref, p_ref, q_ref, a_ref, f_ref, row1, row0, cr_ref, left_ref, right_ref,
    s_ref, sum_p, sum_q, give_ref,
):
    rows, cols = e_ref.shape
    e_row, g_row, a_row = halo_of(row_pick(parity("cross") == 0, row0[:ROWS], row1[:ROWS]))
    for start, step in windows(rows):
        inner = slice(start, start + step)
        grad = derive(window(e_ref, e_row, start, step), 0)
        slope = window(a_ref, a_row, start, step)
        around = slice(max(start - ROWS, 0), min(start + step + ROWS, rows))
        total = with_ring((2.0 - f_ref[around, :]) * p_ref[around, :], g_row, start, step, rows)
        total -= 0.5 * slope * grad
        sum_p[inner, :] = total[ROWS : ROWS + step]
        change = derive(total, 0)[ROWS : ROWS + step]
        slope = a_ref[inner, :]
        grad = derive(e_ref[inner, :], 1)
        total = (2.0 - f_ref[inner, :]) * q_ref[inner, :] - 0.5 * slope * grad
        sum_q[inner, :] = total
        lane = place(total.shape, LANES, 1)
        change += jnp.where((lane >= 4) & (lane < cols - 4), derive(total, 1), 0.0)
        s_ref[inner, :] = 0.5 * e_ref[inner, :] - jnp.where(slope > 0.0, 0.125 * change, 0.0)
    give_ref[...] = halves(1 - parity("cross"), left_ref, right_ref, cr_ref, s_ref)


def surface_kernel(
    e_ref, q_ref, a_ref, f_ref, s_in, sum_in, give_in, col1, col0, cr_ref, left_ref, right_ref,
    s_ref, sum_q, give_ref,
):
    rows, cols = e_ref.shape
    even_row, even_col = parity("cross") == 0, parity("along") == 0
    lane = place((rows, LANES), LANES, 1)
    half = LANES // 2
    first, last = slice(0, LANES), slice(cols - LANES, cols)

    def edges(tile, halo):
        ends = pltpu.roll(tile(last), half, 1)
        beyond = jnp.where(lane < half + ROWS, pltpu.roll(halo, half, 1), halo)
        own = jnp.where(lane < ROWS, tile(first), jnp.where(lane < half - ROWS, 0.0, ends))
        return jnp.where(lane < half, own, beyond)

    e_col, g_col, a_col = halo_of(col_pick(even_col, col0[:ROWS], col1[:ROWS]))
    e = edges(lambda where: e_ref[:, where], e_col)
    slope = edges(lambda where: a_ref[:, where], a_col)
    total = edges(lambda where: (2.0 - f_ref[:, where]) * q_ref[:, where], g_col)
    total -= 0.5 * slope * derive(e, 1)
    change = jnp.where(slope > 0.0, 0.125 * derive(total, 1), 0.0)
    total_last, change_last = pltpu.roll(total, half, 1), pltpu.roll(change, half, 1)
    sum_q[...] = sum_in[...]
    sum_q[:, first] = jnp.where(lane < 2, total, sum_in[:, first])
    sum_q[:, last] = jnp.where(lane >= LANES - 2, total_last, sum_in[:, last])
    s_ref[...] = s_in[...]
    s_ref[:, first] = s_in[:, first] - jnp.where(lane < 4, change, 0.0)
    s_ref[:, last] = s_in[:, last] - jnp.where(lane >= LANES - 4, change_last, 0.0)
    added = split(jnp.where((lane < 4) | ((lane >= half - 4) & (lane < half)), -change, 0.0))
    side = 1 - parity("cross")
    left, thin = half_of(side, left_ref), half_of(side, cr_ref)
    cut = left.shape[0]
    partial = dot_split(split(join(left, thin, 0)), added)
    right = join(right_ref[: half - ROWS, :], right_ref[cols - ROWS :, :], 0)
    right = join(right, right_ref[:half, :], 0)
    give_ref[:cut, :] = give_in[:cut, :] + dot_split(split(partial[:cut]), split(right))
    thin = partial[cut:]
    tail = give_in.shape[0]
    give_ref[cut:tail, :] = give_in[cut:, :]
    at = lane[: tail - cut]
    give_ref[cut:tail, first] += jnp.where(at < 4, thin, 0.0)
    give_ref[cut:tail, last] += jnp.where(at >= LANES - 4, pltpu.roll(thin, half, 1), 0.0)
    both = turn_back(even_col, col0[ROWS:], col1[ROWS:])
    picks = lane_pick(both[:ROWS]), lane_pick(both[rows - ROWS :])
    up, down = (join(pick(4, 0), pick(2, 4), 1) for pick in picks)
    give_ref[tail:, :] = jnp.where(even_row, join(down, up, 0), join(up, down, 0))


def half_of(side, ref):
    count = ref.shape[0] // 2
    return ref[pl.ds(pl.multiple_of(side * count, count), count), :]


def halves(side, left_ref, right_ref, cr_ref, s_ref):
    s = split(s_ref[...])
    product = split(dot_split(s, split(right_ref[...])))
    core = dot_split(split(half_of(side, left_ref)), product)
    return join(core, dot_split(split(half_of(side, cr_ref)), s), 0)


def product_kernel(
    s_ref, r_ref, cr_ref, left_ref, right_ref, s_hbm, keep_ref, range_ref, sems
):
    copies = start(pieces(s_ref, s_hbm, sems))
    keep_ref[...] = halves(parity("cross"), left_ref, right_ref, cr_ref, s_ref)
    range_ref[...] = dot(s_ref[...], r_ref[...])
    for copy in copies:
        copy.wait()


def start(copies):
    for copy in copies:
        copy.start()
    return copies


def pieces(source, to, sems, count=4):
    part = source.shape[0] // count
    blocks = [pl.ds(i * part, part) for i in range(count)]
    return [
        pltpu.make_async_copy(source.at[block, :], to.at[block, :], sems.at[i])
        for i, block in enumerate(blocks)
    ]


def merge_kernel(half, keep_ref, got_ref, range_ref, out, across_ref):
    ends = keep_ref.shape[0]
    both = keep_ref[...] + got_ref[:ends]
    at = 0
    for part in (both[:half], range_ref[...]):
        per = tile_count(part) // out.shape[0]
        for k, tile in enumerate(tiles_of(part)):
            out[k // per, at + k % per] = tile
        at += per
    across_ref[...] = join(both[half:], got_ref[ends + ROWS :], 0)


def tile_count(part):
    return part.shape[0] // ROWS * (part.shape[1] // LANES)


def tile_slices(shape):
    return [
        (slice(i, i + ROWS), slice(j, j + LANES))
        for i in range(0, shape[0], ROWS)
        for j in range(0, shape[1], LANES)
    ]


def tiles_of(part):
    return [part[where] for where in tile_slices(part.shape)]


def sum_kernel(crosses, alongs, cuts, got, *rest):
    out = rest[-1]
    first, second = cuts
    count = crosses * alongs

    def add(values):
        values = list(values)
        while len(values) > 1:
            values = [sum(values[i : i + 2][1:], values[i]) for i in range(0, len(values), 2)]
        return values[0]

    for t in range(first):
        value = add(got[k, t] for k in range(count))
        for k in range(count):
            out[k, t] = value
    for t in range(first, second):
        for c in range(crosses):
            value = add(got[c * alongs + a, t] for a in range(alongs))
            for a in range(alongs):
                out[c * alongs + a, t] = value


def unpack_kernel(mine, theirs, thin_mine, thin_theirs, *refs):
    outs, held, sems = refs[:3], refs[3:6], refs[6]
    core, ranged, coranged = held
    count = mine.shape[0]
    even = parity("cross") == 0
    thin = thin_mine.shape[0]
    coranged[:thin] = jnp.where(even, thin_mine[...], thin_theirs[...])
    coranged[thin:] = jnp.where(even, thin_theirs[...], thin_mine[...])
    copies = start(pieces(coranged, outs[2], sems.at[2]))
    places = tile_slices(ranged.shape)
    wide = len(tile_slices(core.shape)) // 2 // count
    per = len(places) // count
    for k, where in enumerate(places):
        ranged[where] = mine[k // per, wide + k % per]
    copies += start(pieces(ranged, outs[1], sems.at[1]))
    places = tile_slices(core.shape)
    keep = len(places) // 2
    for k in range(keep):
        tile, other = mine[k // wide, k % wide], theirs[k // wide, k % wide]
        core[places[k]] = jnp.where(even, tile, other)
        core[places[keep + k]] = jnp.where(even, other, tile)
    copies += start(pieces(core, outs[0], sems.at[0]))
    for copy in copies:
        copy.wait()


def both_kernel(
    e_ref, mp_ref, mq_ref, a_ref, row1, row0, col1, col0, after,
    both_ref, both_row, both_col, quarter_row, quarter_col,
):
    del after
    rows, cols = e_ref.shape
    even_row, even_col = parity("cross") == 0, parity("along") == 0
    pick = row_pick(even_row, row0[:ROWS], row1[:ROWS])
    e_row, a_row = pick(4, 0), pick(2, 6)
    pick = row_pick(even_row, row0[ROWS:], row1[ROWS:])
    p_row, q_row = pick(4, 0), pick(2, 4)
    pick = col_pick(even_col, col0[:ROWS], col1[:ROWS])
    e_col, a_col = pick(4, 0), pick(2, 6)
    pick = col_pick(even_col, col0[ROWS:], col1[ROWS:])
    q_col, p_col = pick(4, 0), pick(2, 4)
    quarter_row[...] = jnp.where(a_row > 0.0, 0.25, 0.0)
    quarter_col[...] = jnp.where(a_col > 0.0, 0.25, 0.0)
    none = jnp.zeros((ROWS, LANES), e_ref.dtype)
    ends = []
    for start, step in windows(rows):

        def ring(tile, row, col):
            return join(window(tile, row, start, step), window(col, none, start, step), 1)

        spread = derive(ring(mp_ref, p_row, p_col), 0) + derive(ring(mq_ref, q_row, q_col), 1)
        wet = ring(a_ref, a_row, a_col) > 0.0
        both = ring(e_ref, e_row, e_col) - jnp.where(wet, 0.25 * spread, 0.0)
        inner = slice(start, start + step)
        both_ref[inner, :] = both[ROWS : ROWS + step, :cols]
        both_col[inner, :] = both[ROWS : ROWS + step, cols:]
        ends += [both[:ROWS, :cols], both[ROWS + step :, :cols]]
    at = place((ROWS, cols), ROWS, 0)
    both_row[...] = jnp.where(at < ROWS // 2, ends[-1], ends[0])


def flux_kernel(
    both_ref, both_row, both_col, quarter_row, quarter_col, a_ref, f_ref, got_ref, corner_ref,
    p_ref, q_ref, sum_p, sum_q, p_hbm, q_hbm, next_p, next_q, sems,
):
    rows, cols = both_ref.shape
    copies = []
    row = lax.axis_index("cross")
    inside = (row > 0) & (row < lax.axis_size("cross") - 1)
    beyond = jnp.where(inside, corner_ref[corner_ref.shape[0] - ROWS :], 0.0)
    near = got_ref.shape[0] - 2 * ROWS
    pick = row_pick(parity("cross") == 0, got_ref[near : near + ROWS], beyond)
    corners = pick(2, 0)
    dtype = both_ref.dtype
    extra = derive(join(jnp.zeros((ROWS, cols), dtype), corners[:, :LANES], 1), 1)[:, :cols]
    rim_rows = both_row[...] - quarter_row[...] * extra
    extra = derive(join(jnp.zeros((rows, LANES), dtype), corners[:, LANES:], 0), 0)[:rows]
    rim_cols = both_col[...] - quarter_col[...] * extra
    for i, (start, step) in enumerate(windows(rows)):
        inner = slice(start, start + step)
        grad_x = derive(window(both_ref, rim_rows, start, step), 0)[ROWS : ROWS + step]
        grad_y = derive(join(both_ref[inner, :], rim_cols[inner], 1), 1)[:, :cols]
        slope, friction = 0.5 * a_ref[inner, :], 0.5 * f_ref[inner, :]
        next_p[inner, :] = p_ref[inner, :] - (slope * grad_x + friction * sum_p[inner, :])
        next_q[inner, :] = q_ref[inner, :] - (slope * grad_y + friction * sum_q[inner, :])
        for k, (ref, hbm) in enumerate(((next_p, p_hbm), (next_q, q_hbm))):
            copy = pltpu.make_async_copy(ref.at[inner, :], hbm.at[inner, :], sems.at[k, i])
            copy.start()
            copies.append(copy)
    for copy in copies:
        copy.wait()


def pairs_from(start, count):
    pairs = [(i, i + 1) for i in range(start, count - 1, 2)]
    return pairs + [(j, i) for i, j in pairs]


def swap(message, axis, start):
    pairs = pairs_from(start, lax.axis_size(axis))
    return lax.ppermute(message, axis, pairs) if pairs else jnp.zeros_like(message)


def body(e, p, q, c, w, range_test, corange_test, core_left, core_right):
    crosses, alongs = lax.axis_size("cross"), lax.axis_size("along")
    rows, cols = e.shape
    cells = rows * cols

    def run(kernel, outs, flops, *args, idle=(), scratch=(), to=None, space=pltpu.VMEM, limit=32 << 20):
        kinds = [pl.BlockSpec(memory_space=space)] * len(args)
        kinds += [pl.BlockSpec(memory_space=pl.ANY)] * len(idle)
        moved = sum(a.size * 4 for a in args) + sum(o.size * 4 for o in outs)
        to = to or [pltpu.VMEM] * len(outs)
        return pl.pallas_call(
            kernel,
            out_shape=outs,
            in_specs=kinds,
            out_specs=[pl.BlockSpec(memory_space=kind) for kind in to],
            scratch_shapes=list(scratch),
            cost_estimate=pl.CostEstimate(flops=flops, bytes_accessed=moved, transcendentals=0),
            compiler_params=pltpu.CompilerParams(vmem_limit_bytes=limit),
        )(*args, *idle)

    held = [pltpu.VMEM((2, ROWS, cols), a.dtype) for a in (e, p, q, c, w)]
    row0, row1 = run(
        row_kernel, [f32(2 * ROWS, cols)] * 2, cells, e, p, q, c, w, space=pltpu.HBM,
        scratch=held + [pltpu.SemaphoreType.DMA((5, 2))], limit=ROOM,
    )
    row1, row0 = swap(row1, "cross", 1), swap(row0, "cross", 0)
    tile = f32(rows, cols)
    *fields, col0, col1 = run(
        col_kernel, [tile] * 5 + [f32(2 * ROWS, rows)] * 2, 10 * cells, e, p, q, c, w
    )
    col1, col0 = swap(col1, "along", 1), swap(col0, "along", 0)
    halo = (row1, row0, col1, col0)
    range_shape = f32(rows, range_test.shape[1])
    corange_shape = f32(corange_test.shape[0], cols)
    core_shape = f32(core_left.shape[0], core_right.shape[1])
    half, thin = core_shape.shape[0] // 2, corange_shape.shape[0] // 2
    e2, mass_x, mass_y, slope, friction = fields
    row1, row0, col1, col0 = halo
    tests = (corange_test, core_left, core_right)
    s_part, sum_p, sum_q, give = run(
        inner_kernel, [tile] * 3 + [f32(half + thin, cols)], 600 * cells,
        *fields, row1, row0, *tests,
    )
    outs = [tile] * 2 + [f32(half + thin + 2 * ROWS, cols)]
    s_held, sum_q, give = run(
        surface_kernel, outs, 200 * cells,
        e2, mass_y, slope, friction, s_part, sum_q, give, col1, col0, *tests,
    )
    got = swap(give, "cross", 0)
    count = crosses // 2 * alongs
    sizes = (half * core_shape.shape[1], range_shape.size)
    keep_shape = f32(half + thin, cols)
    s_next, keep, ranged = run(
        product_kernel, [tile, keep_shape, range_shape], 300 * cells,
        s_held, range_test, *tests,
        to=[pltpu.HBM, pltpu.VMEM, pltpu.VMEM], scratch=[pltpu.SemaphoreType.DMA((4,))],
    )
    rim_shapes = [tile] + [f32(ROWS, cols), f32(rows, LANES)] * 2
    shared = crosses == 4 and not any(size % (count * ROWS * LANES) for size in sizes)
    if shared:
        per = [size // (count * ROWS * LANES) for size in sizes]
        cuts = (per[0], per[0] + per[1])
        sheet = f32(count, cuts[1], ROWS, LANES)
        groups = [
            [i * alongs + a for i in range(side, crosses, 2) for a in range(alongs)]
            for side in range(2)
        ]

        def spread(x):
            return lax.all_to_all(x, AXES, 0, 0, tiled=True, axis_index_groups=groups)

        shares, across = run(
            functools.partial(merge_kernel, half), [sheet, f32(thin + ROWS, cols)], sheet.size,
            keep, got, ranged,
        )
        rims = run(both_kernel, rim_shapes, 60 * cells, e2, mass_x, mass_y, slope, *halo, across)
        corner = lax.ppermute(across, "cross", [(i, i ^ 2) for i in range(crosses)])
        thin_mine = across[:thin] + corner[:thin]
        thin_theirs = swap(thin_mine, "cross", 0)
        (totals,) = run(
            functools.partial(sum_kernel, crosses // 2, alongs, cuts), [sheet], sheet.size,
            spread(shares), idle=[thin_mine, rims[1]],
        )
        mine = spread(totals)
        theirs = swap(mine, "cross", 0)
        shapes = [core_shape, range_shape, corange_shape]
        core, ranged, coranged = run(
            unpack_kernel, shapes, sheet.size, mine, theirs, thin_mine, thin_theirs,
            to=[pltpu.HBM] * 3,
            scratch=[pltpu.VMEM(x.shape, x.dtype) for x in shapes]
            + [pltpu.SemaphoreType.DMA((3, 4))],
        )
    else:
        corner = swap(give[-ROWS:], "cross", 1)
        rims = run(both_kernel, rim_shapes, 60 * cells, e2, mass_x, mass_y, slope, *halo, give)
        ranged = lax.psum(ranged, "along")
        coranged = lax.psum(dot(corange_test, s_held), "cross")
        core = lax.psum(dot(core_left, dot(s_held, core_right)), AXES)
    p_next, q_next = run(
        flux_kernel, [tile] * 2, 40 * cells,
        *rims, slope, friction, got, corner, p, q, sum_p, sum_q,
        to=[pltpu.HBM] * 2,
        scratch=[pltpu.VMEM((rows, cols), jnp.float32)] * 2
        + [pltpu.SemaphoreType.DMA((2, len(list(windows(rows)))))],
    )
    return s_next, p_next, q_next, ranged, coranged, core


def solution(mesh):
    tile = P("cross", "along")
    return jax.shard_map(
        body,
        mesh=mesh,
        in_specs=(tile,) * 5
        + (P("along", None), P(None, "cross"), P(None, "cross"), P("along", None)),
        out_specs=(tile,) * 3 + (P("cross", None), P(None, "along"), P()),
        check_vma=False,
    )
```

```python
import functools

import jax
import jax.numpy as jnp
from jax import lax
from jax.experimental import pallas as pl
from jax.experimental.pallas import tpu as pltpu
from jax.sharding import PartitionSpec as P

AXES = ("cross", "along")
ROWS = 8
LANES = 128
WINDOW = 64
ROOM = 56_450_000


def f32(*shape):
    return jax.ShapeDtypeStruct(shape, jnp.float32)


def derive(field, axis):
    size = field.shape[axis]

    def part(shift):
        return pltpu.roll(field, (-shift) % size, axis)

    return (part(1) - part(-1)) * (8.0 / 12.0) - (part(2) - part(-2)) * (1.0 / 12.0)


def friction_of(slope):
    wet = slope > 0.0
    return jnp.where(wet, 0.005 / jnp.where(wet, slope, 1.0), 0.0)


def place(shape, axis, dim):
    return lax.broadcasted_iota(jnp.int32, shape, dim)


def parity(axis):
    return lax.rem(lax.axis_index(axis), 2)


def row_kernel(e_hbm, p_hbm, q_hbm, c_hbm, w_hbm, first_ref, second_ref, eb, pb, qb, cb, wb, sems):
    rows, cols = e_hbm.shape
    copies = [
        pltpu.make_async_copy(source.at[pl.ds(i * (rows - ROWS), ROWS), :], to.at[i], sems.at[k, i])
        for k, (source, to) in enumerate(
            ((e_hbm, eb), (p_hbm, pb), (q_hbm, qb), (c_hbm, cb), (w_hbm, wb))
        )
        for i in range(2)
    ]
    for copy in copies:
        copy.start()
    for copy in copies:
        copy.wait()
    at = place((ROWS, cols), ROWS, 0)
    messages = []
    for i, (far, near, turn) in enumerate(((at < 4, at < 6, 6), (at >= 4, at >= 2, 2))):
        wet = wb[i] > 0
        slope = jnp.where(wet, 0.25 * cb[i], 0.0)
        mass, side = jnp.where(wet, pb[i], 0.0), jnp.where(wet, qb[i], 0.0)
        first = jnp.where(near, pltpu.roll(mass, 4, 0), pltpu.roll(slope, turn, 0))
        first = jnp.where(far, 2.0 * eb[i], first)
        messages.append(join(first, jnp.where(far, mass, pltpu.roll(side, 4, 0)), 0))
    up, down = messages
    even = parity("cross") == 0
    first_ref[...] = jnp.where(even, down, up)
    second_ref[...] = jnp.where(even, up, down)


def col_kernel(e_ref, p_ref, q_ref, c_ref, w_ref, first_ref, second_ref):
    rows, cols = e_ref.shape
    lane = place((rows, LANES), LANES, 1)
    left = lane < LANES // 2
    off = jnp.minimum(lane, LANES - 1 - lane)

    def edge(ref):
        return jnp.where(left, ref[:, :LANES], ref[:, cols - LANES :])

    def shift(block, count):
        return jnp.where(left, pltpu.roll(block, count, 1), pltpu.roll(block, LANES - count, 1))

    wet = edge(w_ref) > 0
    slope = jnp.where(wet, 0.25 * edge(c_ref), 0.0)
    mass, side = jnp.where(wet, edge(q_ref), 0.0), jnp.where(wet, edge(p_ref), 0.0)
    first = jnp.where(off < 4, 2.0 * edge(e_ref), jnp.where(off < 6, shift(mass, 4), shift(slope, 6))).T
    second = jnp.where(off < 4, mass, shift(side, 4)).T
    to_left = join(first[:ROWS], second[:ROWS], 0)
    to_right = join(first[LANES - ROWS :], second[LANES - ROWS :], 0)
    even = parity("along") == 0
    first_ref[...] = jnp.where(even, to_right, to_left)
    second_ref[...] = jnp.where(even, to_left, to_right)


def row_pick(even, first, second):
    below, above = jnp.where(even, first, second), jnp.where(even, second, first)
    at = place(below.shape, ROWS, 0)

    def pick(count, shift):
        low = pltpu.roll(below, ROWS - shift, 0) if shift else below
        high = pltpu.roll(above, shift, 0) if shift else above
        return jnp.where(at < count, low, jnp.where(at >= ROWS - count, high, 0.0))

    return pick


def turn_back(even, first, second):
    right, left = jnp.where(even, first, second), jnp.where(even, second, first)
    gap = jnp.zeros((LANES - 2 * ROWS, right.shape[1]), right.dtype)
    return jnp.concatenate([right, gap, left], axis=0).T


def lane_pick(both):
    lane = place(both.shape, LANES, 1)

    def pick(count, shift):
        low = pltpu.roll(both, LANES - shift, 1) if shift else both
        high = pltpu.roll(both, shift, 1) if shift else both
        return jnp.where(lane < count, low, jnp.where(lane >= LANES - count, high, 0.0))

    return pick


def col_pick(even, first, second):
    return lane_pick(turn_back(even, first, second))


def split(a):
    high = a.astype(jnp.bfloat16)
    return high, (a - high.astype(jnp.float32)).astype(jnp.bfloat16)


def dot_split(a, b):
    (a_high, a_low), (b_high, b_low) = a, b

    def product(x, y):
        return jnp.dot(x, y, preferred_element_type=jnp.float32)

    return product(a_high, b_high) + (product(a_high, b_low) + product(a_low, b_high))


def dot(a, b):
    return dot_split(split(a), split(b))


def join(tile, halo, axis):
    return jnp.concatenate([tile, halo], axis=axis)


def windows(rows):
    step = WINDOW if rows % WINDOW == 0 else ROWS
    for start in range(0, rows, step):
        yield start, step


def with_ring(part, ring, start, step, rows):
    parts = [part]
    if start == 0:
        parts.insert(0, ring)
    if start + step == rows:
        parts.append(ring)
    return jnp.concatenate(parts, axis=0) if len(parts) > 1 else part


def window(tile, ring, start, step):
    rows = tile.shape[0]
    part = tile[max(start - ROWS, 0) : min(start + step + ROWS, rows)]
    return with_ring(part, ring, start, step, rows)


def halo_of(pick):
    e, mass, slope = pick(4, 0), pick(2, 4), pick(2, 6)
    return e, (2.0 - friction_of(slope)) * mass, slope


def inner_kernel(
    e_in, p_in, q_in, c_in, w_in, row1, row0, cr_ref, left_ref, right_ref,
    e_ref, p_ref, q_ref, a_ref, f_ref, s_ref, sum_p, sum_q, give_ref,
):
    rows, cols = e_ref.shape
    for start, step in windows(rows):
        here = slice(start, start + step)
        wet, celerity_sq = w_in[here, :] > 0, c_in[here, :]
        e_ref[here, :] = 2.0 * e_in[here, :]
        p_ref[here, :] = jnp.where(wet, p_in[here, :], 0.0)
        q_ref[here, :] = jnp.where(wet, q_in[here, :], 0.0)
        a_ref[here, :] = jnp.where(wet, 0.25 * celerity_sq, 0.0)
        f_ref[here, :] = jnp.where(wet, 0.02 / celerity_sq, 0.0)
    e_row, g_row, a_row = halo_of(row_pick(parity("cross") == 0, row0[:ROWS], row1[:ROWS]))
    for start, step in windows(rows):
        inner = slice(start, start + step)
        grad = derive(window(e_ref, e_row, start, step), 0)
        slope = window(a_ref, a_row, start, step)
        around = slice(max(start - ROWS, 0), min(start + step + ROWS, rows))
        total = with_ring((2.0 - f_ref[around, :]) * p_ref[around, :], g_row, start, step, rows)
        total -= 0.5 * slope * grad
        sum_p[inner, :] = total[ROWS : ROWS + step]
        change = derive(total, 0)[ROWS : ROWS + step]
        slope = a_ref[inner, :]
        grad = derive(e_ref[inner, :], 1)
        total = (2.0 - f_ref[inner, :]) * q_ref[inner, :] - 0.5 * slope * grad
        sum_q[inner, :] = total
        lane = place(total.shape, LANES, 1)
        change += jnp.where((lane >= 4) & (lane < cols - 4), derive(total, 1), 0.0)
        s_ref[inner, :] = 0.5 * e_ref[inner, :] - jnp.where(slope > 0.0, 0.125 * change, 0.0)
    give_ref[...] = halves(1 - parity("cross"), left_ref, right_ref, cr_ref, s_ref)


def surface_kernel(
    e_ref, q_ref, a_ref, f_ref, s_in, sum_in, give_in, col1, col0, cr_ref, left_ref, right_ref,
    s_ref, sum_q, give_ref,
):
    rows, cols = e_ref.shape
    even_row, even_col = parity("cross") == 0, parity("along") == 0
    lane = place((rows, LANES), LANES, 1)
    half = LANES // 2
    first, last = slice(0, LANES), slice(cols - LANES, cols)

    def edges(tile, halo):
        ends = pltpu.roll(tile(last), half, 1)
        beyond = jnp.where(lane < half + ROWS, pltpu.roll(halo, half, 1), halo)
        own = jnp.where(lane < ROWS, tile(first), jnp.where(lane < half - ROWS, 0.0, ends))
        return jnp.where(lane < half, own, beyond)

    e_col, g_col, a_col = halo_of(col_pick(even_col, col0[:ROWS], col1[:ROWS]))
    e = edges(lambda where: e_ref[:, where], e_col)
    slope = edges(lambda where: a_ref[:, where], a_col)
    total = edges(lambda where: (2.0 - f_ref[:, where]) * q_ref[:, where], g_col)
    total -= 0.5 * slope * derive(e, 1)
    change = jnp.where(slope > 0.0, 0.125 * derive(total, 1), 0.0)
    total_last, change_last = pltpu.roll(total, half, 1), pltpu.roll(change, half, 1)
    sum_q[...] = sum_in[...]
    sum_q[:, first] = jnp.where(lane < 2, total, sum_in[:, first])
    sum_q[:, last] = jnp.where(lane >= LANES - 2, total_last, sum_in[:, last])
    s_ref[...] = s_in[...]
    s_ref[:, first] = s_in[:, first] - jnp.where(lane < 4, change, 0.0)
    s_ref[:, last] = s_in[:, last] - jnp.where(lane >= LANES - 4, change_last, 0.0)
    added = split(jnp.where((lane < 4) | ((lane >= half - 4) & (lane < half)), -change, 0.0))
    side = 1 - parity("cross")
    left, thin = half_of(side, left_ref), half_of(side, cr_ref)
    cut = left.shape[0]
    partial = dot_split(split(join(left, thin, 0)), added)
    right = join(right_ref[: half - ROWS, :], right_ref[cols - ROWS :, :], 0)
    right = join(right, right_ref[:half, :], 0)
    give_ref[:cut, :] = give_in[:cut, :] + dot_split(split(partial[:cut]), split(right))
    thin = partial[cut:]
    tail = give_in.shape[0]
    give_ref[cut:tail, :] = give_in[cut:, :]
    at = lane[: tail - cut]
    give_ref[cut:tail, first] += jnp.where(at < 4, thin, 0.0)
    give_ref[cut:tail, last] += jnp.where(at >= LANES - 4, pltpu.roll(thin, half, 1), 0.0)
    both = turn_back(even_col, col0[ROWS:], col1[ROWS:])
    picks = lane_pick(both[:ROWS]), lane_pick(both[rows - ROWS :])
    up, down = (join(pick(4, 0), pick(2, 4), 1) for pick in picks)
    give_ref[tail:, :] = jnp.where(even_row, join(down, up, 0), join(up, down, 0))


def half_of(side, ref):
    count = ref.shape[0] // 2
    return ref[pl.ds(pl.multiple_of(side * count, count), count), :]


def halves(side, left_ref, right_ref, cr_ref, s_ref):
    s = split(s_ref[...])
    product = split(dot_split(s, split(right_ref[...])))
    core = dot_split(split(half_of(side, left_ref)), product)
    return join(core, dot_split(split(half_of(side, cr_ref)), s), 0)


def product_kernel(
    s_ref, r_ref, cr_ref, left_ref, right_ref, s_hbm, keep_ref, range_ref, sems
):
    copies = start(pieces(s_ref, s_hbm, sems))
    keep_ref[...] = halves(parity("cross"), left_ref, right_ref, cr_ref, s_ref)
    range_ref[...] = dot(s_ref[...], r_ref[...])
    for copy in copies:
        copy.wait()


def start(copies):
    for copy in copies:
        copy.start()
    return copies


def pieces(source, to, sems, count=4):
    part = source.shape[0] // count
    blocks = [pl.ds(i * part, part) for i in range(count)]
    return [
        pltpu.make_async_copy(source.at[block, :], to.at[block, :], sems.at[i])
        for i, block in enumerate(blocks)
    ]


def merge_kernel(half, keep_ref, got_ref, range_ref, out, across_ref):
    ends = keep_ref.shape[0]
    both = keep_ref[...] + got_ref[:ends]
    at = 0
    for part in (both[:half], range_ref[...]):
        per = tile_count(part) // out.shape[0]
        for k, tile in enumerate(tiles_of(part)):
            out[k // per, at + k % per] = tile
        at += per
    across_ref[...] = join(both[half:], got_ref[ends + ROWS :], 0)


def tile_count(part):
    return part.shape[0] // ROWS * (part.shape[1] // LANES)


def tile_slices(shape):
    return [
        (slice(i, i + ROWS), slice(j, j + LANES))
        for i in range(0, shape[0], ROWS)
        for j in range(0, shape[1], LANES)
    ]


def tiles_of(part):
    return [part[where] for where in tile_slices(part.shape)]


def sum_kernel(crosses, alongs, cuts, got, *rest):
    out = rest[-1]
    first, second = cuts
    count = crosses * alongs

    def add(values):
        values = list(values)
        while len(values) > 1:
            values = [sum(values[i : i + 2][1:], values[i]) for i in range(0, len(values), 2)]
        return values[0]

    for t in range(first):
        value = add(got[k, t] for k in range(count))
        for k in range(count):
            out[k, t] = value
    for t in range(first, second):
        for c in range(crosses):
            value = add(got[c * alongs + a, t] for a in range(alongs))
            for a in range(alongs):
                out[c * alongs + a, t] = value


def unpack_kernel(mine, core_hbm, range_hbm, core, ranged, sems):
    wide = unpack_core(mine, core)
    copies = start(pieces(core, rows_of(core_hbm, parity("cross")), sems.at[0]))
    places = tile_slices(ranged.shape)
    per = len(places) // mine.shape[0]
    for k, where in enumerate(places):
        ranged[where] = mine[k // per, wide + k % per]
    copies += start(pieces(ranged, range_hbm, sems.at[1]))
    for copy in copies:
        copy.wait()


def unpack_core(handed, core):
    places = tile_slices(core.shape)
    wide = len(places) // handed.shape[0]
    for k, where in enumerate(places):
        core[where] = handed[k // wide, k % wide]
    return wide


def rows_of(ref, side):
    count = ref.shape[0] // 2
    return ref.at[pl.ds(pl.multiple_of(side * count, count), count), :]


def complete_kernel(theirs, core_in, thin_mine, thin_theirs, core_hbm, corange_hbm,
                    core, coranged, sems):
    del core_in
    unpack_core(theirs, core)
    copies = start(pieces(core, rows_of(core_hbm, 1 - parity("cross")), sems.at[0]))
    thin = thin_mine.shape[0]
    even = parity("cross") == 0
    coranged[:thin] = jnp.where(even, thin_mine[...], thin_theirs[...])
    coranged[thin:] = jnp.where(even, thin_theirs[...], thin_mine[...])
    copies += start(pieces(coranged, corange_hbm, sems.at[1]))
    for copy in copies:
        copy.wait()


def both_kernel(
    e_ref, mp_ref, mq_ref, a_ref, row1, row0, col1, col0, after,
    both_ref, both_row, both_col, quarter_row, quarter_col,
):
    del after
    rows, cols = e_ref.shape
    even_row, even_col = parity("cross") == 0, parity("along") == 0
    pick = row_pick(even_row, row0[:ROWS], row1[:ROWS])
    e_row, a_row = pick(4, 0), pick(2, 6)
    pick = row_pick(even_row, row0[ROWS:], row1[ROWS:])
    p_row, q_row = pick(4, 0), pick(2, 4)
    pick = col_pick(even_col, col0[:ROWS], col1[:ROWS])
    e_col, a_col = pick(4, 0), pick(2, 6)
    pick = col_pick(even_col, col0[ROWS:], col1[ROWS:])
    q_col, p_col = pick(4, 0), pick(2, 4)
    quarter_row[...] = jnp.where(a_row > 0.0, 0.25, 0.0)
    quarter_col[...] = jnp.where(a_col > 0.0, 0.25, 0.0)
    none = jnp.zeros((ROWS, LANES), e_ref.dtype)
    ends = []
    for start, step in windows(rows):

        def ring(tile, row, col):
            return join(window(tile, row, start, step), window(col, none, start, step), 1)

        spread = derive(ring(mp_ref, p_row, p_col), 0) + derive(ring(mq_ref, q_row, q_col), 1)
        wet = ring(a_ref, a_row, a_col) > 0.0
        both = ring(e_ref, e_row, e_col) - jnp.where(wet, 0.25 * spread, 0.0)
        inner = slice(start, start + step)
        both_ref[inner, :] = both[ROWS : ROWS + step, :cols]
        both_col[inner, :] = both[ROWS : ROWS + step, cols:]
        ends += [both[:ROWS, :cols], both[ROWS + step :, :cols]]
    at = place((ROWS, cols), ROWS, 0)
    both_row[...] = jnp.where(at < ROWS // 2, ends[-1], ends[0])


def flux_kernel(
    both_ref, both_row, both_col, quarter_row, quarter_col, a_ref, f_ref, got_ref, corner_ref,
    p_ref, q_ref, sum_p, sum_q, p_hbm, q_hbm, token, next_p, next_q, sems,
):
    rows, cols = both_ref.shape
    token[...] = jnp.zeros(token.shape, token.dtype)
    copies = []
    row = lax.axis_index("cross")
    inside = (row > 0) & (row < lax.axis_size("cross") - 1)
    beyond = jnp.where(inside, corner_ref[corner_ref.shape[0] - ROWS :], 0.0)
    near = got_ref.shape[0] - 2 * ROWS
    pick = row_pick(parity("cross") == 0, got_ref[near : near + ROWS], beyond)
    corners = pick(2, 0)
    dtype = both_ref.dtype
    extra = derive(join(jnp.zeros((ROWS, cols), dtype), corners[:, :LANES], 1), 1)[:, :cols]
    rim_rows = both_row[...] - quarter_row[...] * extra
    extra = derive(join(jnp.zeros((rows, LANES), dtype), corners[:, LANES:], 0), 0)[:rows]
    rim_cols = both_col[...] - quarter_col[...] * extra
    for i, (start, step) in enumerate(windows(rows)):
        inner = slice(start, start + step)
        grad_x = derive(window(both_ref, rim_rows, start, step), 0)[ROWS : ROWS + step]
        grad_y = derive(join(both_ref[inner, :], rim_cols[inner], 1), 1)[:, :cols]
        slope, friction = 0.5 * a_ref[inner, :], 0.5 * f_ref[inner, :]
        next_p[inner, :] = p_ref[inner, :] - (slope * grad_x + friction * sum_p[inner, :])
        next_q[inner, :] = q_ref[inner, :] - (slope * grad_y + friction * sum_q[inner, :])
        for k, (ref, hbm) in enumerate(((next_p, p_hbm), (next_q, q_hbm))):
            copy = pltpu.make_async_copy(ref.at[inner, :], hbm.at[inner, :], sems.at[k, i])
            copy.start()
            copies.append(copy)
    for copy in copies:
        copy.wait()


def pairs_from(start, count):
    pairs = [(i, i + 1) for i in range(start, count - 1, 2)]
    return pairs + [(j, i) for i, j in pairs]


def swap(message, axis, start):
    pairs = pairs_from(start, lax.axis_size(axis))
    return lax.ppermute(message, axis, pairs) if pairs else jnp.zeros_like(message)


def body(e, p, q, c, w, range_test, corange_test, core_left, core_right):
    crosses, alongs = lax.axis_size("cross"), lax.axis_size("along")
    rows, cols = e.shape
    cells = rows * cols

    def run(kernel, outs, flops, *args, idle=(), scratch=(), to=None, space=pltpu.VMEM, limit=32 << 20,
            alias=None):
        kinds = [pl.BlockSpec(memory_space=space)] * len(args)
        for i in alias or {}:
            kinds[i] = pl.BlockSpec(memory_space=pltpu.HBM)
        kinds += [pl.BlockSpec(memory_space=pl.ANY)] * len(idle)
        moved = sum(a.size * 4 for a in args) + sum(o.size * 4 for o in outs)
        to = to or [pltpu.VMEM] * len(outs)
        return pl.pallas_call(
            kernel,
            out_shape=outs,
            in_specs=kinds,
            out_specs=[pl.BlockSpec(memory_space=kind) for kind in to],
            scratch_shapes=list(scratch),
            input_output_aliases=alias or {},
            cost_estimate=pl.CostEstimate(flops=flops, bytes_accessed=moved, transcendentals=0),
            compiler_params=pltpu.CompilerParams(vmem_limit_bytes=limit),
        )(*args, *idle)

    held = [pltpu.VMEM((2, ROWS, cols), a.dtype) for a in (e, p, q, c, w)]
    row0, row1 = run(
        row_kernel, [f32(2 * ROWS, cols)] * 2, cells, e, p, q, c, w, space=pltpu.HBM,
        scratch=held + [pltpu.SemaphoreType.DMA((5, 2))], limit=ROOM,
    )
    row1, row0 = swap(row1, "cross", 1), swap(row0, "cross", 0)
    tile = f32(rows, cols)
    col0, col1 = run(col_kernel, [f32(2 * ROWS, rows)] * 2, 10 * cells, e, p, q, c, w)
    col1, col0 = swap(col1, "along", 1), swap(col0, "along", 0)
    halo = (row1, row0, col1, col0)
    range_shape = f32(rows, range_test.shape[1])
    corange_shape = f32(corange_test.shape[0], cols)
    core_shape = f32(core_left.shape[0], core_right.shape[1])
    half, thin = core_shape.shape[0] // 2, corange_shape.shape[0] // 2
    row1, row0, col1, col0 = halo
    tests = (corange_test, core_left, core_right)
    e2, mass_x, mass_y, slope, friction, s_part, sum_p, sum_q, give = run(
        inner_kernel, [tile] * 8 + [f32(half + thin, cols)], 600 * cells,
        e, p, q, c, w, row1, row0, *tests,
    )
    outs = [tile] * 2 + [f32(half + thin + 2 * ROWS, cols)]
    s_held, sum_q, give = run(
        surface_kernel, outs, 200 * cells,
        e2, mass_y, slope, friction, s_part, sum_q, give, col1, col0, *tests,
    )
    got = swap(give, "cross", 0)
    count = crosses // 2 * alongs
    sizes = (half * core_shape.shape[1], range_shape.size)
    keep_shape = f32(half + thin, cols)
    s_next, keep, ranged = run(
        product_kernel, [tile, keep_shape, range_shape], 300 * cells,
        s_held, range_test, *tests,
        to=[pltpu.HBM, pltpu.VMEM, pltpu.VMEM], scratch=[pltpu.SemaphoreType.DMA((4,))],
    )
    rim_shapes = [tile] + [f32(ROWS, cols), f32(rows, LANES)] * 2
    def fluxes(rims, corner):
        return run(
            flux_kernel, [tile] * 2 + [f32(ROWS, LANES)], 40 * cells,
            *rims, slope, friction, got, corner, p, q, sum_p, sum_q,
            to=[pltpu.HBM] * 2 + [pltpu.VMEM],
            scratch=[pltpu.VMEM((rows, cols), jnp.float32)] * 2
            + [pltpu.SemaphoreType.DMA((2, len(list(windows(rows)))))],
        )

    shared = crosses == 4 and not any(size % (count * ROWS * LANES) for size in sizes)
    if shared:
        per = [size // (count * ROWS * LANES) for size in sizes]
        cuts = (per[0], per[0] + per[1])
        sheet = f32(count, cuts[1], ROWS, LANES)
        groups = [
            [i * alongs + a for i in range(side, crosses, 2) for a in range(alongs)]
            for side in range(2)
        ]

        def spread(x):
            return lax.all_to_all(x, AXES, 0, 0, tiled=True, axis_index_groups=groups)

        shares, across = run(
            functools.partial(merge_kernel, half), [sheet, f32(thin + ROWS, cols)], sheet.size,
            keep, got, ranged,
        )
        rims = run(both_kernel, rim_shapes, 60 * cells, e2, mass_x, mass_y, slope, *halo, across)
        corner = lax.ppermute(across, "cross", [(i, i ^ 2) for i in range(crosses)])
        thin_mine = across[:thin] + corner[:thin]
        thin_theirs = swap(thin_mine, "cross", 0)
        p_next, q_next, token = fluxes(rims, corner)
        (totals,) = run(
            functools.partial(sum_kernel, crosses // 2, alongs, cuts), [sheet], sheet.size,
            spread(shares), idle=[thin_mine, token],
        )
        mine = spread(totals)
        theirs = swap(mine, "cross", 0)
        held = [f32(half, core_shape.shape[1]), range_shape, corange_shape]
        held = [pltpu.VMEM(x.shape, x.dtype) for x in held]
        core, ranged = run(
            unpack_kernel, [core_shape, range_shape], sheet.size, mine,
            to=[pltpu.HBM] * 2, scratch=held[:2] + [pltpu.SemaphoreType.DMA((2, 4))],
        )
        core, coranged = run(
            complete_kernel, [core_shape, corange_shape], sheet.size,
            theirs, core, thin_mine, thin_theirs, to=[pltpu.HBM] * 2, alias={1: 0},
            scratch=[held[0], held[2], pltpu.SemaphoreType.DMA((2, 4))],
        )
    else:
        corner = swap(give[-ROWS:], "cross", 1)
        rims = run(both_kernel, rim_shapes, 60 * cells, e2, mass_x, mass_y, slope, *halo, give)
        p_next, q_next, _ = fluxes(rims, corner)
        ranged = lax.psum(ranged, "along")
        coranged = lax.psum(dot(corange_test, s_held), "cross")
        core = lax.psum(dot(core_left, dot(s_held, core_right)), AXES)
    return s_next, p_next, q_next, ranged, coranged, core


def solution(mesh):
    tile = P("cross", "along")
    return jax.shard_map(
        body,
        mesh=mesh,
        in_specs=(tile,) * 5
        + (P("along", None), P(None, "cross"), P(None, "cross"), P("along", None)),
        out_specs=(tile,) * 3 + (P("cross", None), P(None, "along"), P()),
        check_vma=False,
    )
```

```python
import functools

import jax
import jax.numpy as jnp
from jax import lax
from jax.experimental import pallas as pl
from jax.experimental.pallas import tpu as pltpu
from jax.sharding import PartitionSpec as P

AXES = ("cross", "along")
ROWS = 8
LANES = 128
WINDOW = 64
ROOM = 56_450_000


def f32(*shape):
    return jax.ShapeDtypeStruct(shape, jnp.float32)


def derive(field, axis):
    size = field.shape[axis]

    def part(shift):
        return pltpu.roll(field, (-shift) % size, axis)

    return (part(1) - part(-1)) * (8.0 / 12.0) - (part(2) - part(-2)) * (1.0 / 12.0)


def friction_of(slope):
    wet = slope > 0.0
    return jnp.where(wet, 0.005 / jnp.where(wet, slope, 1.0), 0.0)


def place(shape, axis, dim):
    return lax.broadcasted_iota(jnp.int32, shape, dim)


def parity(axis):
    return lax.rem(lax.axis_index(axis), 2)


def row_kernel(e_hbm, p_hbm, q_hbm, c_hbm, w_hbm, first_ref, second_ref, eb, pb, qb, cb, wb, sems):
    rows, cols = e_hbm.shape
    copies = [
        pltpu.make_async_copy(source.at[pl.ds(i * (rows - ROWS), ROWS), :], to.at[i], sems.at[k, i])
        for k, (source, to) in enumerate(
            ((e_hbm, eb), (p_hbm, pb), (q_hbm, qb), (c_hbm, cb), (w_hbm, wb))
        )
        for i in range(2)
    ]
    for copy in copies:
        copy.start()
    for copy in copies:
        copy.wait()
    at = place((ROWS, cols), ROWS, 0)
    messages = []
    for i, (far, near, turn) in enumerate(((at < 4, at < 6, 6), (at >= 4, at >= 2, 2))):
        wet = wb[i] > 0
        slope = jnp.where(wet, 0.25 * cb[i], 0.0)
        mass, side = jnp.where(wet, pb[i], 0.0), jnp.where(wet, qb[i], 0.0)
        first = jnp.where(near, pltpu.roll(mass, 4, 0), pltpu.roll(slope, turn, 0))
        first = jnp.where(far, 2.0 * eb[i], first)
        messages.append(join(first, jnp.where(far, mass, pltpu.roll(side, 4, 0)), 0))
    up, down = messages
    even = parity("cross") == 0
    first_ref[...] = jnp.where(even, down, up)
    second_ref[...] = jnp.where(even, up, down)


def col_kernel(e_ref, p_ref, q_ref, c_ref, w_ref, first_ref, second_ref):
    rows, cols = e_ref.shape
    lane = place((rows, LANES), LANES, 1)
    left = lane < LANES // 2
    off = jnp.minimum(lane, LANES - 1 - lane)

    def edge(ref):
        return jnp.where(left, ref[:, :LANES], ref[:, cols - LANES :])

    def shift(block, count):
        return jnp.where(left, pltpu.roll(block, count, 1), pltpu.roll(block, LANES - count, 1))

    wet = edge(w_ref) > 0
    slope = jnp.where(wet, 0.25 * edge(c_ref), 0.0)
    mass, side = jnp.where(wet, edge(q_ref), 0.0), jnp.where(wet, edge(p_ref), 0.0)
    first = jnp.where(off < 4, 2.0 * edge(e_ref), jnp.where(off < 6, shift(mass, 4), shift(slope, 6))).T
    second = jnp.where(off < 4, mass, shift(side, 4)).T
    to_left = join(first[:ROWS], second[:ROWS], 0)
    to_right = join(first[LANES - ROWS :], second[LANES - ROWS :], 0)
    even = parity("along") == 0
    first_ref[...] = jnp.where(even, to_right, to_left)
    second_ref[...] = jnp.where(even, to_left, to_right)


def row_pick(even, first, second):
    below, above = jnp.where(even, first, second), jnp.where(even, second, first)
    at = place(below.shape, ROWS, 0)

    def pick(count, shift):
        low = pltpu.roll(below, ROWS - shift, 0) if shift else below
        high = pltpu.roll(above, shift, 0) if shift else above
        return jnp.where(at < count, low, jnp.where(at >= ROWS - count, high, 0.0))

    return pick


def turn_back(even, first, second):
    right, left = jnp.where(even, first, second), jnp.where(even, second, first)
    gap = jnp.zeros((LANES - 2 * ROWS, right.shape[1]), right.dtype)
    return jnp.concatenate([right, gap, left], axis=0).T


def lane_pick(both):
    lane = place(both.shape, LANES, 1)

    def pick(count, shift):
        low = pltpu.roll(both, LANES - shift, 1) if shift else both
        high = pltpu.roll(both, shift, 1) if shift else both
        return jnp.where(lane < count, low, jnp.where(lane >= LANES - count, high, 0.0))

    return pick


def col_pick(even, first, second):
    return lane_pick(turn_back(even, first, second))


def split(a):
    high = a.astype(jnp.bfloat16)
    return high, (a - high.astype(jnp.float32)).astype(jnp.bfloat16)


def dot_split(a, b):
    (a_high, a_low), (b_high, b_low) = a, b

    def product(x, y):
        return jnp.dot(x, y, preferred_element_type=jnp.float32)

    return product(a_high, b_high) + (product(a_high, b_low) + product(a_low, b_high))


def dot(a, b):
    return dot_split(split(a), split(b))


def join(tile, halo, axis):
    return jnp.concatenate([tile, halo], axis=axis)


def windows(rows):
    step = WINDOW if rows % WINDOW == 0 else ROWS
    for start in range(0, rows, step):
        yield start, step


def with_ring(part, ring, start, step, rows):
    parts = [part]
    if start == 0:
        parts.insert(0, ring)
    if start + step == rows:
        parts.append(ring)
    return jnp.concatenate(parts, axis=0) if len(parts) > 1 else part


def window(tile, ring, start, step):
    rows = tile.shape[0]
    part = tile[max(start - ROWS, 0) : min(start + step + ROWS, rows)]
    return with_ring(part, ring, start, step, rows)


def halo_of(pick):
    e, mass, slope = pick(4, 0), pick(2, 4), pick(2, 6)
    return e, (2.0 - friction_of(slope)) * mass, slope


def inner_kernel(
    e_in, p_in, q_in, c_in, w_in, row1, row0, cr_ref, left_ref, right_ref,
    e_ref, p_ref, q_ref, a_ref, f_ref, s_ref, sum_p, sum_q, give_ref,
):
    rows, cols = e_ref.shape
    for start, step in windows(rows):
        here = slice(start, start + step)
        wet, celerity_sq = w_in[here, :] > 0, c_in[here, :]
        e_ref[here, :] = 2.0 * e_in[here, :]
        p_ref[here, :] = jnp.where(wet, p_in[here, :], 0.0)
        q_ref[here, :] = jnp.where(wet, q_in[here, :], 0.0)
        a_ref[here, :] = jnp.where(wet, 0.25 * celerity_sq, 0.0)
        f_ref[here, :] = jnp.where(wet, 0.02 / celerity_sq, 0.0)
    e_row, g_row, a_row = halo_of(row_pick(parity("cross") == 0, row0[:ROWS], row1[:ROWS]))
    for start, step in windows(rows):
        inner = slice(start, start + step)
        grad = derive(window(e_ref, e_row, start, step), 0)
        slope = window(a_ref, a_row, start, step)
        around = slice(max(start - ROWS, 0), min(start + step + ROWS, rows))
        total = with_ring((2.0 - f_ref[around, :]) * p_ref[around, :], g_row, start, step, rows)
        total -= 0.5 * slope * grad
        sum_p[inner, :] = total[ROWS : ROWS + step]
        change = derive(total, 0)[ROWS : ROWS + step]
        slope = a_ref[inner, :]
        grad = derive(e_ref[inner, :], 1)
        total = (2.0 - f_ref[inner, :]) * q_ref[inner, :] - 0.5 * slope * grad
        sum_q[inner, :] = total
        lane = place(total.shape, LANES, 1)
        change += jnp.where((lane >= 4) & (lane < cols - 4), derive(total, 1), 0.0)
        s_ref[inner, :] = 0.5 * e_ref[inner, :] - jnp.where(slope > 0.0, 0.125 * change, 0.0)
    give_ref[...] = halves(1 - parity("cross"), left_ref, right_ref, cr_ref, s_ref)


def surface_kernel(
    e_ref, q_ref, a_ref, f_ref, s_in, sum_in, give_in, col1, col0, cr_ref, left_ref, right_ref,
    s_ref, sum_q, give_ref,
):
    rows, cols = e_ref.shape
    even_row, even_col = parity("cross") == 0, parity("along") == 0
    lane = place((rows, LANES), LANES, 1)
    half = LANES // 2
    first, last = slice(0, LANES), slice(cols - LANES, cols)

    def edges(tile, halo):
        ends = pltpu.roll(tile(last), half, 1)
        beyond = jnp.where(lane < half + ROWS, pltpu.roll(halo, half, 1), halo)
        own = jnp.where(lane < ROWS, tile(first), jnp.where(lane < half - ROWS, 0.0, ends))
        return jnp.where(lane < half, own, beyond)

    e_col, g_col, a_col = halo_of(col_pick(even_col, col0[:ROWS], col1[:ROWS]))
    e = edges(lambda where: e_ref[:, where], e_col)
    slope = edges(lambda where: a_ref[:, where], a_col)
    total = edges(lambda where: (2.0 - f_ref[:, where]) * q_ref[:, where], g_col)
    total -= 0.5 * slope * derive(e, 1)
    change = jnp.where(slope > 0.0, 0.125 * derive(total, 1), 0.0)
    total_last, change_last = pltpu.roll(total, half, 1), pltpu.roll(change, half, 1)
    sum_q[...] = sum_in[...]
    sum_q[:, first] = jnp.where(lane < 2, total, sum_in[:, first])
    sum_q[:, last] = jnp.where(lane >= LANES - 2, total_last, sum_in[:, last])
    s_ref[...] = s_in[...]
    s_ref[:, first] = s_in[:, first] - jnp.where(lane < 4, change, 0.0)
    s_ref[:, last] = s_in[:, last] - jnp.where(lane >= LANES - 4, change_last, 0.0)
    added = split(jnp.where((lane < 4) | ((lane >= half - 4) & (lane < half)), -change, 0.0))
    side = 1 - parity("cross")
    left, thin = half_of(side, left_ref), half_of(side, cr_ref)
    cut = left.shape[0]
    partial = dot_split(split(join(left, thin, 0)), added)
    right = join(right_ref[: half - ROWS, :], right_ref[cols - ROWS :, :], 0)
    right = join(right, right_ref[:half, :], 0)
    give_ref[:cut, :] = give_in[:cut, :] + dot_split(split(partial[:cut]), split(right))
    thin = partial[cut:]
    tail = give_in.shape[0]
    give_ref[cut:tail, :] = give_in[cut:, :]
    at = lane[: tail - cut]
    give_ref[cut:tail, first] += jnp.where(at < 4, thin, 0.0)
    give_ref[cut:tail, last] += jnp.where(at >= LANES - 4, pltpu.roll(thin, half, 1), 0.0)
    both = turn_back(even_col, col0[ROWS:], col1[ROWS:])
    picks = lane_pick(both[:ROWS]), lane_pick(both[rows - ROWS :])
    up, down = (join(pick(4, 0), pick(2, 4), 1) for pick in picks)
    give_ref[tail:, :] = jnp.where(even_row, join(down, up, 0), join(up, down, 0))


def half_of(side, ref):
    count = ref.shape[0] // 2
    return ref[pl.ds(pl.multiple_of(side * count, count), count), :]


def halves(side, left_ref, right_ref, cr_ref, s_ref):
    s = split(s_ref[...])
    product = split(dot_split(s, split(right_ref[...])))
    core = dot_split(split(half_of(side, left_ref)), product)
    return join(core, dot_split(split(half_of(side, cr_ref)), s), 0)


def product_kernel(
    s_ref, r_ref, cr_ref, left_ref, right_ref, keep_ref, range_ref
):
    keep_ref[...] = halves(parity("cross"), left_ref, right_ref, cr_ref, s_ref)
    range_ref[...] = dot(s_ref[...], r_ref[...])


def start(copies):
    for copy in copies:
        copy.start()
    return copies


def pieces(source, to, sems, count=4):
    part = source.shape[0] // count
    blocks = [pl.ds(i * part, part) for i in range(count)]
    return [
        pltpu.make_async_copy(source.at[block, :], to.at[block, :], sems.at[i])
        for i, block in enumerate(blocks)
    ]


def merge_kernel(half, keep_ref, got_ref, range_ref, out, across_ref):
    ends = keep_ref.shape[0]
    both = keep_ref[...] + got_ref[:ends]
    at = 0
    for part in (both[:half], range_ref[...]):
        per = tile_count(part) // out.shape[0]
        for k, tile in enumerate(tiles_of(part)):
            out[k // per, at + k % per] = tile
        at += per
    across_ref[...] = join(both[half:], got_ref[ends + ROWS :], 0)


def tile_count(part):
    return part.shape[0] // ROWS * (part.shape[1] // LANES)


def tile_slices(shape):
    return [
        (slice(i, i + ROWS), slice(j, j + LANES))
        for i in range(0, shape[0], ROWS)
        for j in range(0, shape[1], LANES)
    ]


def tiles_of(part):
    return [part[where] for where in tile_slices(part.shape)]


def sum_kernel(crosses, alongs, cuts, got, *rest):
    out = rest[-1]
    first, second = cuts
    count = crosses * alongs

    def add(values):
        values = list(values)
        while len(values) > 1:
            values = [sum(values[i : i + 2][1:], values[i]) for i in range(0, len(values), 2)]
        return values[0]

    for t in range(first):
        value = add(got[k, t] for k in range(count))
        for k in range(count):
            out[k, t] = value
    for t in range(first, second):
        for c in range(crosses):
            value = add(got[c * alongs + a, t] for a in range(alongs))
            for a in range(alongs):
                out[c * alongs + a, t] = value


def unpack_kernel(mine, core_hbm, range_hbm, core, ranged, sems):
    wide = unpack_core(mine, core)
    copies = start(pieces(core, rows_of(core_hbm, parity("cross")), sems.at[0]))
    places = tile_slices(ranged.shape)
    per = len(places) // mine.shape[0]
    for k, where in enumerate(places):
        ranged[where] = mine[k // per, wide + k % per]
    copies += start(pieces(ranged, range_hbm, sems.at[1]))
    for copy in copies:
        copy.wait()


def unpack_core(handed, core):
    places = tile_slices(core.shape)
    wide = len(places) // handed.shape[0]
    for k, where in enumerate(places):
        core[where] = handed[k // wide, k % wide]
    return wide


def rows_of(ref, side):
    count = ref.shape[0] // 2
    return ref.at[pl.ds(pl.multiple_of(side * count, count), count), :]


def complete_kernel(theirs, core_in, thin_mine, thin_theirs, core_hbm, corange_hbm,
                    core, coranged, sems):
    del core_in
    unpack_core(theirs, core)
    copies = start(pieces(core, rows_of(core_hbm, 1 - parity("cross")), sems.at[0]))
    thin = thin_mine.shape[0]
    even = parity("cross") == 0
    coranged[:thin] = jnp.where(even, thin_mine[...], thin_theirs[...])
    coranged[thin:] = jnp.where(even, thin_theirs[...], thin_mine[...])
    copies += start(pieces(coranged, corange_hbm, sems.at[1]))
    for copy in copies:
        copy.wait()


def both_kernel(
    e_ref, mp_ref, mq_ref, a_ref, row1, row0, col1, col0, s_ref, after,
    both_ref, both_row, both_col, quarter_row, quarter_col, s_hbm, sems,
):
    del after
    copies = pieces(s_ref, s_hbm, sems)
    for copy in copies:
        copy.start()
    rows, cols = e_ref.shape
    even_row, even_col = parity("cross") == 0, parity("along") == 0
    pick = row_pick(even_row, row0[:ROWS], row1[:ROWS])
    e_row, a_row = pick(4, 0), pick(2, 6)
    pick = row_pick(even_row, row0[ROWS:], row1[ROWS:])
    p_row, q_row = pick(4, 0), pick(2, 4)
    pick = col_pick(even_col, col0[:ROWS], col1[:ROWS])
    e_col, a_col = pick(4, 0), pick(2, 6)
    pick = col_pick(even_col, col0[ROWS:], col1[ROWS:])
    q_col, p_col = pick(4, 0), pick(2, 4)
    quarter_row[...] = jnp.where(a_row > 0.0, 0.25, 0.0)
    quarter_col[...] = jnp.where(a_col > 0.0, 0.25, 0.0)
    none = jnp.zeros((ROWS, LANES), e_ref.dtype)
    ends = []
    for start, step in windows(rows):

        def ring(tile, row, col):
            return join(window(tile, row, start, step), window(col, none, start, step), 1)

        spread = derive(ring(mp_ref, p_row, p_col), 0) + derive(ring(mq_ref, q_row, q_col), 1)
        wet = ring(a_ref, a_row, a_col) > 0.0
        both = ring(e_ref, e_row, e_col) - jnp.where(wet, 0.25 * spread, 0.0)
        inner = slice(start, start + step)
        both_ref[inner, :] = both[ROWS : ROWS + step, :cols]
        both_col[inner, :] = both[ROWS : ROWS + step, cols:]
        ends += [both[:ROWS, :cols], both[ROWS + step :, :cols]]
    at = place((ROWS, cols), ROWS, 0)
    both_row[...] = jnp.where(at < ROWS // 2, ends[-1], ends[0])
    for copy in copies:
        copy.wait()


def flux_kernel(
    both_ref, both_row, both_col, quarter_row, quarter_col, a_ref, f_ref, got_ref, corner_ref,
    p_ref, q_ref, sum_p, sum_q, p_hbm, q_hbm, token, next_p, next_q, sems,
):
    rows, cols = both_ref.shape
    token[...] = jnp.zeros(token.shape, token.dtype)
    copies = []
    row = lax.axis_index("cross")
    inside = (row > 0) & (row < lax.axis_size("cross") - 1)
    beyond = jnp.where(inside, corner_ref[corner_ref.shape[0] - ROWS :], 0.0)
    near = got_ref.shape[0] - 2 * ROWS
    pick = row_pick(parity("cross") == 0, got_ref[near : near + ROWS], beyond)
    corners = pick(2, 0)
    dtype = both_ref.dtype
    extra = derive(join(jnp.zeros((ROWS, cols), dtype), corners[:, :LANES], 1), 1)[:, :cols]
    rim_rows = both_row[...] - quarter_row[...] * extra
    extra = derive(join(jnp.zeros((rows, LANES), dtype), corners[:, LANES:], 0), 0)[:rows]
    rim_cols = both_col[...] - quarter_col[...] * extra
    for i, (start, step) in enumerate(windows(rows)):
        inner = slice(start, start + step)
        grad_x = derive(window(both_ref, rim_rows, start, step), 0)[ROWS : ROWS + step]
        grad_y = derive(join(both_ref[inner, :], rim_cols[inner], 1), 1)[:, :cols]
        slope, friction = 0.5 * a_ref[inner, :], 0.5 * f_ref[inner, :]
        next_p[inner, :] = p_ref[inner, :] - (slope * grad_x + friction * sum_p[inner, :])
        next_q[inner, :] = q_ref[inner, :] - (slope * grad_y + friction * sum_q[inner, :])
        for k, (ref, hbm) in enumerate(((next_p, p_hbm), (next_q, q_hbm))):
            copy = pltpu.make_async_copy(ref.at[inner, :], hbm.at[inner, :], sems.at[k, i])
            copy.start()
            copies.append(copy)
    for copy in copies:
        copy.wait()


def pairs_from(start, count):
    pairs = [(i, i + 1) for i in range(start, count - 1, 2)]
    return pairs + [(j, i) for i, j in pairs]


def swap(message, axis, start):
    pairs = pairs_from(start, lax.axis_size(axis))
    return lax.ppermute(message, axis, pairs) if pairs else jnp.zeros_like(message)


def body(e, p, q, c, w, range_test, corange_test, core_left, core_right):
    crosses, alongs = lax.axis_size("cross"), lax.axis_size("along")
    rows, cols = e.shape
    cells = rows * cols

    def run(kernel, outs, flops, *args, idle=(), scratch=(), to=None, space=pltpu.VMEM, limit=32 << 20,
            alias=None):
        kinds = [pl.BlockSpec(memory_space=space)] * len(args)
        for i in alias or {}:
            kinds[i] = pl.BlockSpec(memory_space=pltpu.HBM)
        kinds += [pl.BlockSpec(memory_space=pl.ANY)] * len(idle)
        moved = sum(a.size * 4 for a in args) + sum(o.size * 4 for o in outs)
        to = to or [pltpu.VMEM] * len(outs)
        return pl.pallas_call(
            kernel,
            out_shape=outs,
            in_specs=kinds,
            out_specs=[pl.BlockSpec(memory_space=kind) for kind in to],
            scratch_shapes=list(scratch),
            input_output_aliases=alias or {},
            cost_estimate=pl.CostEstimate(flops=flops, bytes_accessed=moved, transcendentals=0),
            compiler_params=pltpu.CompilerParams(vmem_limit_bytes=limit),
        )(*args, *idle)

    held = [pltpu.VMEM((2, ROWS, cols), a.dtype) for a in (e, p, q, c, w)]
    row0, row1 = run(
        row_kernel, [f32(2 * ROWS, cols)] * 2, cells, e, p, q, c, w, space=pltpu.HBM,
        scratch=held + [pltpu.SemaphoreType.DMA((5, 2))], limit=ROOM,
    )
    row1, row0 = swap(row1, "cross", 1), swap(row0, "cross", 0)
    tile = f32(rows, cols)
    col0, col1 = run(col_kernel, [f32(2 * ROWS, rows)] * 2, 10 * cells, e, p, q, c, w)
    col1, col0 = swap(col1, "along", 1), swap(col0, "along", 0)
    halo = (row1, row0, col1, col0)
    range_shape = f32(rows, range_test.shape[1])
    corange_shape = f32(corange_test.shape[0], cols)
    core_shape = f32(core_left.shape[0], core_right.shape[1])
    half, thin = core_shape.shape[0] // 2, corange_shape.shape[0] // 2
    row1, row0, col1, col0 = halo
    tests = (corange_test, core_left, core_right)
    e2, mass_x, mass_y, slope, friction, s_part, sum_p, sum_q, give = run(
        inner_kernel, [tile] * 8 + [f32(half + thin, cols)], 600 * cells,
        e, p, q, c, w, row1, row0, *tests,
    )
    outs = [tile] * 2 + [f32(half + thin + 2 * ROWS, cols)]
    s_held, sum_q, give = run(
        surface_kernel, outs, 200 * cells,
        e2, mass_y, slope, friction, s_part, sum_q, give, col1, col0, *tests,
    )
    got = swap(give, "cross", 0)
    count = crosses // 2 * alongs
    sizes = (half * core_shape.shape[1], range_shape.size)
    keep_shape = f32(half + thin, cols)
    keep, ranged = run(
        product_kernel, [keep_shape, range_shape], 300 * cells, s_held, range_test, *tests
    )
    rim_shapes = [tile] + [f32(ROWS, cols), f32(rows, LANES)] * 2

    def beside(after):
        *rims, s_next = run(
            both_kernel, rim_shapes + [tile], 60 * cells,
            e2, mass_x, mass_y, slope, *halo, s_held, after,
            to=[pltpu.VMEM] * 5 + [pltpu.HBM], scratch=[pltpu.SemaphoreType.DMA((4,))],
        )
        return rims, s_next

    def fluxes(rims, corner):
        return run(
            flux_kernel, [tile] * 2 + [f32(ROWS, LANES)], 40 * cells,
            *rims, slope, friction, got, corner, p, q, sum_p, sum_q,
            to=[pltpu.HBM] * 2 + [pltpu.VMEM],
            scratch=[pltpu.VMEM((rows, cols), jnp.float32)] * 2
            + [pltpu.SemaphoreType.DMA((2, len(list(windows(rows)))))],
        )

    shared = crosses == 4 and not any(size % (count * ROWS * LANES) for size in sizes)
    if shared:
        per = [size // (count * ROWS * LANES) for size in sizes]
        cuts = (per[0], per[0] + per[1])
        sheet = f32(count, cuts[1], ROWS, LANES)
        groups = [
            [i * alongs + a for i in range(side, crosses, 2) for a in range(alongs)]
            for side in range(2)
        ]

        def spread(x):
            return lax.all_to_all(x, AXES, 0, 0, tiled=True, axis_index_groups=groups)

        shares, across = run(
            functools.partial(merge_kernel, half), [sheet, f32(thin + ROWS, cols)], sheet.size,
            keep, got, ranged,
        )
        rims, s_next = beside(across)
        corner = lax.ppermute(across, "cross", [(i, i ^ 2) for i in range(crosses)])
        thin_mine = across[:thin] + corner[:thin]
        thin_theirs = swap(thin_mine, "cross", 0)
        p_next, q_next, token = fluxes(rims, corner)
        (totals,) = run(
            functools.partial(sum_kernel, crosses // 2, alongs, cuts), [sheet], sheet.size,
            spread(shares), idle=[thin_mine, token],
        )
        mine = spread(totals)
        theirs = swap(mine, "cross", 0)
        held = [f32(half, core_shape.shape[1]), range_shape, corange_shape]
        held = [pltpu.VMEM(x.shape, x.dtype) for x in held]
        core, ranged = run(
            unpack_kernel, [core_shape, range_shape], sheet.size, mine,
            to=[pltpu.HBM] * 2, scratch=held[:2] + [pltpu.SemaphoreType.DMA((2, 4))],
        )
        core, coranged = run(
            complete_kernel, [core_shape, corange_shape], sheet.size,
            theirs, core, thin_mine, thin_theirs, to=[pltpu.HBM] * 2, alias={1: 0},
            scratch=[held[0], held[2], pltpu.SemaphoreType.DMA((2, 4))],
        )
    else:
        corner = swap(give[-ROWS:], "cross", 1)
        rims, s_next = beside(give)
        p_next, q_next, _ = fluxes(rims, corner)
        ranged = lax.psum(ranged, "along")
        coranged = lax.psum(dot(corange_test, s_held), "cross")
        core = lax.psum(dot(core_left, dot(s_held, core_right)), AXES)
    return s_next, p_next, q_next, ranged, coranged, core


def solution(mesh):
    tile = P("cross", "along")
    return jax.shard_map(
        body,
        mesh=mesh,
        in_specs=(tile,) * 5
        + (P("along", None), P(None, "cross"), P(None, "cross"), P("along", None)),
        out_specs=(tile,) * 3 + (P("cross", None), P(None, "along"), P()),
        check_vma=False,
    )
```
